256 devices in a mesh: row: 8 (over y, core), col: 32 (over x, z).
Axes of the slice: x: 4, y: 4, z: 8, core: 2. Of those that a mesh axis runs over, the one named last changes fastest.
Arguments:
- attn_grad: float32 [4, 4096, 4096], P(None, 'row', 'col'), may hold values from -54 to 54
- attn_param: float32 [4, 4096, 4096], P(None, 'row', 'col'), may hold values from -150 to 150
- attn_rows: float32 [4, 4096], P(None, 'row'), may hold values from 0.03 to 0.3
- attn_cols: float32 [4, 4096], P(None, 'col'), may hold values from 0.03 to 0.3
- wi_grad: float32 [2, 4096, 10240], P(None, 'row', 'col'), may hold values from -54 to 54
- wi_param: float32 [2, 4096, 10240], P(None, 'row', 'col'), may hold values from -150 to 150
- wi_rows: float32 [2, 4096], P(None, 'row'), may hold values from 4 to 40
- wi_cols: float32 [2, 10240], P(None, 'col'), may hold values from 4 to 40
- wo_grad: float32 [10240, 4096], P('row', 'col'), may hold values from -54 to 54
- wo_param: float32 [10240, 4096], P('row', 'col'), may hold values from -150 to 150
- wo_rows: float32 [10240], P('row'), may hold values from 4 to 40
- wo_cols: float32 [4096], P('col'), may hold values from 4 to 40
Outputs:
- attn_update: float32 [4, 4096, 4096], P(None, 'row', 'col')
- attn_rows_new: float32 [4, 4096], P(None, 'row')
- attn_cols_new: float32 [4, 4096], P(None, 'col')
- wi_update: float32 [2, 4096, 10240], P(None, 'row', 'col')
- wi_rows_new: float32 [2, 4096], P(None, 'row')
- wi_cols_new: float32 [2, 10240], P(None, 'col')
- wo_update: float32 [10240, 4096], P('row', 'col')
- wo_rows_new: float32 [10240], P('row')
- wo_cols_new: float32 [4096], P('col')
The draws below stay inside these ranges and needn't reach their ends.
All inputs are finite; a program needn't handle non-finite values.
Results may differ from the reference program's by a relative error of at most 0.00002.
Values sent between devices are 32-bit elements; how exact they have to be, the bound alone decides.
No kernel may reach another device: no remote copies, remote signals or barrier semaphores. Data moves between devices by JAX's collectives and lax.ppermute only.
A program may use at most 64 MiB of HBM per device.

```python
import math
import jax
import jax.numpy as jnp
from jax import lax

D = 4096
INNER = 4096
FF = 10240
ATTN_MATS = 4
STEP = 2


def outer_scales(key, shape, low, high):
    key_row, key_col = jax.random.split(key)
    row_shape = shape[:-1] + (1,)
    col_shape = shape[:-2] + (1, shape[-1])
    row_scale = jnp.exp(jax.random.uniform(key_row, row_shape, jnp.float32, math.log(low), math.log(high)))
    col_scale = jnp.exp(jax.random.uniform(key_col, col_shape, jnp.float32, math.log(low), math.log(high)))
    return row_scale * col_scale


def normal_entries(key, shape):
    return jnp.clip(jax.random.normal(key, shape, jnp.float32), -6.0, 6.0)


def grad_field(key, shape):
    key_base, key_scale = jax.random.split(key)
    return (normal_entries(key_base, shape) * outer_scales(key_scale, shape, 0.3, 3.0)).astype(jnp.float32)


def param_field(key, shape):
    key_base, key_scale = jax.random.split(key)
    return (normal_entries(key_base, shape) * outer_scales(key_scale, shape, 0.5, 5.0)).astype(jnp.float32)


def draw_attn_grad(key, part):
    key = jax.random.fold_in(key, 11)
    return grad_field(key, (ATTN_MATS, D, INNER))


def draw_attn_param(key, part):
    key = jax.random.fold_in(key, 12)
    return param_field(key, (ATTN_MATS, D, INNER))


def draw_wi_grad(key, part):
    key = jax.random.fold_in(key, 13)
    return grad_field(key, (2, D, FF))


def draw_wi_param(key, part):
    key = jax.random.fold_in(key, 14)
    return param_field(key, (2, D, FF))


def draw_wo_grad(key, part):
    key = jax.random.fold_in(key, 15)
    return grad_field(key, (FF, D))


def draw_wo_param(key, part):
    key = jax.random.fold_in(key, 16)
    return param_field(key, (FF, D))


def block_levels(key, extent, pieces, low, high):
    loudness, own = 1.0, jax.random.fold_in(key, 6)
    for position, parts in pieces:
        heights = jnp.exp(jax.random.uniform(jax.random.fold_in(own, position), (parts,), jnp.float32, low / len(pieces), high / len(pieces)))
        loudness = loudness * jnp.repeat(heights, extent[position] // parts).reshape([-1 if axis == position else 1 for axis in range(len(extent))])
    return loudness


def setup_inputs(seed: int = 0) -> dict:
    keys = jax.random.split(jax.random.key(seed), 13)
    return {
        "attn_grad": draw_attn_grad(jax.random.fold_in(keys[12], 71), 0),
        "attn_param": draw_attn_param(jax.random.fold_in(keys[12], 71), 0),
        "attn_rows": jnp.clip(jnp.exp(math.log(0.3) - 2.3025852 * jax.random.uniform(keys[2], (ATTN_MATS, D), jnp.float32) ** block_levels(keys[2], (ATTN_MATS, D), ((1, 8),), -0.2, 0.2)), 0.03, 0.3),
        "attn_cols": jnp.clip(jnp.exp(math.log(0.3) - 2.3025852 * jax.random.uniform(keys[3], (ATTN_MATS, INNER), jnp.float32) ** block_levels(keys[3], (ATTN_MATS, INNER), ((1, 32),), -0.2, 0.2)), 0.03, 0.3),
        "wi_grad": draw_wi_grad(jax.random.fold_in(keys[12], 71), 0),
        "wi_param": draw_wi_param(jax.random.fold_in(keys[12], 71), 0),
        "wi_rows": jnp.clip(jnp.exp(math.log(40.0) - 2.3025851 * jax.random.uniform(keys[6], (2, D), jnp.float32) ** block_levels(keys[6], (2, D), ((1, 8),), -0.2, 0.2)), 4.0, 40.0),
        "wi_cols": jnp.clip(jnp.exp(math.log(40.0) - 2.3025851 * jax.random.uniform(keys[7], (2, FF), jnp.float32) ** block_levels(keys[7], (2, FF), ((1, 32),), -0.2, 0.2)), 4.0, 40.0),
        "wo_grad": draw_wo_grad(jax.random.fold_in(keys[12], 71), 0),
        "wo_param": draw_wo_param(jax.random.fold_in(keys[12], 71), 0),
        "wo_rows": jnp.clip(jnp.exp(math.log(40.0) - 2.3025851 * jax.random.uniform(keys[10], (FF,), jnp.float32) ** block_levels(keys[10], (FF,), ((0, 8),), -0.2, 0.2)), 4.0, 40.0),
        "wo_cols": jnp.clip(jnp.exp(math.log(40.0) - 2.3025851 * jax.random.uniform(keys[11], (D,), jnp.float32) ** block_levels(keys[11], (D,), ((0, 32),), -0.2, 0.2)), 4.0, 40.0),
    }


EPS_SQUARE = 1e-30

def one_matrix(grad, param, rows, cols):
    beta = 1.0 - STEP ** (-0.8)
    rho = STEP ** (-0.5)
    squares = grad * grad + EPS_SQUARE
    rows_new = beta * rows + (1.0 - beta) * (lax.optimization_barrier(jnp.sum(squares, axis=1)) / squares.shape[1])
    cols_new = beta * cols + (1.0 - beta) * (lax.optimization_barrier(jnp.sum(squares, axis=0)) / squares.shape[0])
    level = jnp.sum(rows_new) / rows_new.shape[0]
    direction = grad * lax.rsqrt(rows_new[:, None] * cols_new[None, :] / level)
    count = squares.shape[0] * squares.shape[1]
    dir_rms = jnp.sqrt(jnp.sum(direction * direction) / count)
    param_rms = jnp.sqrt(jnp.sum(param * param) / count)
    update = -rho * param_rms * direction / jnp.maximum(1.0, dir_rms)
    return (update, rows_new, cols_new)

def stacked(grads, params, rows, cols):
    results = [one_matrix(grads[k], params[k], rows[k], cols[k]) for k in range(grads.shape[0])]
    return (jnp.stack([item[0] for item in results]), jnp.stack([item[1] for item in results]), jnp.stack([item[2] for item in results]))

def reference(attn_grad, attn_param, attn_rows, attn_cols, wi_grad, wi_param, wi_rows, wi_cols, wo_grad, wo_param, wo_rows, wo_cols):
    attn_update, attn_rows_new, attn_cols_new = stacked(attn_grad, attn_param, attn_rows, attn_cols)
    wi_update, wi_rows_new, wi_cols_new = stacked(wi_grad, wi_param, wi_rows, wi_cols)
    wo_update, wo_rows_new, wo_cols_new = one_matrix(wo_grad, wo_param, wo_rows, wo_cols)
    return (attn_update, attn_rows_new, attn_cols_new, wi_update, wi_rows_new, wi_cols_new, wo_update, wo_rows_new, wo_cols_new)
```

```python
import jax
import jax.numpy as jnp
from jax import lax
from jax.sharding import Mesh, PartitionSpec as P

STEP = 2
EPS_SQUARE = 1e-30
LANES = 128
ROW = ("y", "core")
COL = ("x", "z")


def one_shot_sum(x, axes, n):
    sent = jnp.broadcast_to(x[None], (n,) + x.shape)
    return jnp.sum(lax.all_to_all(sent, axes, 0, 0), axis=0)


def pack(parts):
    flat = jnp.concatenate([p.reshape(-1) for p in parts])
    pad = -flat.shape[0] % LANES
    return jnp.pad(flat, (0, pad)).reshape(-1, LANES)


def unpack(packed, shapes):
    flat = packed.reshape(-1)
    out, at = [], 0
    for s in shapes:
        size = 1
        for d in s:
            size *= d
        out.append(flat[at : at + size].reshape(s))
        at += size
    return out


def shards(
    attn_grad,
    attn_param,
    attn_rows,
    attn_cols,
    wi_grad,
    wi_param,
    wi_rows,
    wi_cols,
    wo_grad,
    wo_param,
    wo_rows,
    wo_cols,
):
    beta = 1.0 - STEP ** (-0.8)
    rho = STEP ** (-0.5)
    n_row = lax.axis_size(ROW)
    n_x = lax.axis_size("x")
    n_z = lax.axis_size("z")
    grads = (attn_grad, wi_grad, wo_grad[None])
    params = (attn_param, wi_param, wo_param[None])
    rows_old = (attn_rows, wi_rows, wo_rows[None])
    cols_old = (attn_cols, wi_cols, wo_cols[None])
    full_rows = tuple(g.shape[1] * n_row for g in grads)
    full_cols = tuple(g.shape[2] * n_x * n_z for g in grads)
    col_part = [jnp.sum(g * g + EPS_SQUARE, axis=1) for g in grads]
    col_tot = unpack(one_shot_sum(pack(col_part), ROW, n_row), [c.shape for c in col_part])
    cols_new = [beta * cols_old[k] + (1.0 - beta) * (col_tot[k] / full_rows[k]) for k in range(3)]
    row_part = [jnp.sum(g * g + EPS_SQUARE, axis=2) for g in grads]
    inv_cols = [1.0 / c for c in cols_new]
    scaled = [jnp.sum(g * g * v[:, None, :], axis=2) for g, v in zip(grads, inv_cols)]
    param_part = [jnp.sum(p * p, axis=(1, 2)) for p in params]
    parts = row_part + scaled + param_part
    shapes = [p.shape for p in parts]
    tot = one_shot_sum(pack(parts), "x", n_x)
    tot = unpack(one_shot_sum(tot, "z", n_z), shapes)
    row_tot, scaled_tot, param_col = tot[0:3], tot[3:6], tot[6:9]
    rows_new = [beta * rows_old[k] + (1.0 - beta) * (row_tot[k] / full_cols[k]) for k in range(3)]
    new_sum = [jnp.sum(r, axis=1) for r in rows_new]
    ratio = [jnp.sum(s / r, axis=1) for s, r in zip(scaled_tot, rows_new)]
    scalars = new_sum + ratio + param_col
    shapes = [s.shape for s in scalars]
    tot = unpack(one_shot_sum(pack(scalars), ROW, n_row), shapes)
    updates = []
    for k in range(3):
        count = full_rows[k] * full_cols[k]
        level = tot[k] / full_rows[k]
        dir_rms = jnp.sqrt(level * tot[3 + k] / count)
        param_rms = jnp.sqrt(tot[6 + k] / count)
        factor = -rho * param_rms / jnp.maximum(1.0, dir_rms) * jnp.sqrt(level)
        left = lax.rsqrt(rows_new[k]) * factor[:, None]
        right = lax.rsqrt(cols_new[k])
        updates.append(grads[k] * (left[:, :, None] * right[:, None, :]))
    return (
        updates[0],
        rows_new[0],
        cols_new[0],
        updates[1],
        rows_new[1],
        cols_new[1],
        updates[2][0],
        rows_new[2][0],
        cols_new[2][0],
    )


def solution(mesh):
    fine = Mesh(mesh.devices.reshape(4, 2, 4, 8), ("y", "core", "x", "z"))
    return jax.shard_map(
        shards,
        mesh=fine,
        in_specs=(
            P(None, ROW, COL),
            P(None, ROW, COL),
            P(None, ROW),
            P(None, COL),
            P(None, ROW, COL),
            P(None, ROW, COL),
            P(None, ROW),
            P(None, COL),
            P(ROW, COL),
            P(ROW, COL),
            P(ROW),
            P(COL),
        ),
        out_specs=(
            P(None, ROW, COL),
            P(None, ROW),
            P(None, COL),
            P(None, ROW, COL),
            P(None, ROW),
            P(None, COL),
            P(ROW, COL),
            P(ROW),
            P(COL),
        ),
        check_vma=False,
    )
```

```python
import jax
import jax.numpy as jnp
from jax import lax
from jax.experimental import pallas as pl
from jax.experimental.pallas import tpu as pltpu
from jax.sharding import Mesh, PartitionSpec as P

STEP = 2
EPS_SQUARE = 1e-30
BETA = 1.0 - STEP ** (-0.8)
RHO = STEP ** (-0.5)
LANES = 128
N_MATS = 7

ROW = ("y", "core")
COL = ("x", "zq", "zp")
NEAR = ("x", "zp")
FAR = ("zq",)

A_MATS, A_ROWS = 4, 512
W_MATS, W_COLS, W_ROWS = 2, 320, 512
O_ROWS = 1280
A_TILES, O_TILES, W_TILES = A_ROWS // LANES, O_ROWS // LANES, W_ROWS // LANES
W_COL_TILES = -(-W_COLS // LANES)

C_WI, C_WO, C_ALL = 4, 10, 16
R_WI, R_WO, R_ALL = 16, 24, 34
S_PARAM, S_ALL = 2 * R_ALL, 72

VMEM_LIMIT = 48 * 1024 * 1024
WHOLE = pl.BlockSpec(memory_space=pltpu.VMEM)
ANYWHERE = pl.BlockSpec(memory_space=pl.ANY)


def call(body, out_shape, in_specs, out_specs, scratch=(), bytes_accessed=1 << 20, aliases=None):
    return pl.pallas_call(
        body,
        out_shape=out_shape,
        in_specs=in_specs,
        out_specs=out_specs,
        scratch_shapes=list(scratch),
        input_output_aliases=aliases or {},
        compiler_params=pltpu.CompilerParams(vmem_limit_bytes=VMEM_LIMIT),
        cost_estimate=pl.CostEstimate(flops=4 << 20, bytes_accessed=bytes_accessed, transcendentals=0),
    )


def here(x):
    return pltpu.with_memory_space_constraint(x, pltpu.VMEM)


def far(x):
    return pltpu.with_memory_space_constraint(x, pltpu.HBM)


def f32(*shape):
    return jax.ShapeDtypeStruct(shape, jnp.float32)


def vmem(*shape):
    return pltpu.VMEM(shape, jnp.float32)


def hbm(*shape):
    return pltpu.HBM(shape, jnp.float32)


def grad_copies(sources, targets, sems):
    a, w, o = sources
    a_to, w_to, o_to = targets
    pairs = [(a.at[k], a_to.at[k]) for k in range(A_MATS)]
    pairs += [(w.at[k], w_to.at[k]) for k in range(W_MATS)]
    pairs += [(o, o_to)]
    return [pltpu.make_async_copy(s, t, sems.at[i]) for i, (s, t) in enumerate(pairs)]


def total(x):
    return jnp.sum(x, axis=0, keepdims=True)


def as_column(row):
    return jnp.broadcast_to(row, (LANES, LANES)).T


def load_kernel(a, w, o, send, ga, gw, go, packed, sems):
    copies = grad_copies((a, w, o), (ga, gw, go), sems)
    for c in copies:
        c.start()
    packed[...] = jnp.zeros_like(packed)
    for k in range(A_MATS):
        copies[k].wait()
        g = ga[k]
        packed[k : k + 1, :] = total(g * g + EPS_SQUARE)
    for k in range(W_MATS):
        copies[A_MATS + k].wait()
        for b in range(W_COL_TILES):
            lo, hi = b * LANES, min((b + 1) * LANES, W_COLS)
            folded = jnp.zeros((hi - lo, LANES), jnp.float32)
            for t in range(W_TILES):
                g = gw[k, lo:hi, t * LANES : (t + 1) * LANES]
                folded = folded + (g * g + EPS_SQUARE)
            if hi - lo < LANES:
                folded = jnp.concatenate([folded, jnp.zeros((LANES - hi + lo, LANES), jnp.float32)], axis=0)
            at = C_WI + k * W_COL_TILES + b
            packed[at : at + 1, :] = total(folded.T)
    copies[-1].wait()
    g = go[...]
    packed[C_WO : C_WO + 1, :] = total(g * g + EPS_SQUARE)
    value = packed[...]
    for n in range(send.shape[0]):
        send[n] = value


def wi_places():
    for k in range(W_MATS):
        for b in range(W_COL_TILES):
            lo, hi = b * LANES, min((b + 1) * LANES, W_COLS)
            yield k, C_WI + k * W_COL_TILES + b, lo, hi


def row_places():
    for k in range(A_MATS):
        for t in range(A_TILES):
            yield 0, k, t, k * A_TILES + t
    for k in range(W_MATS):
        for t in range(W_TILES):
            yield 1, k, t, R_WI + k * W_TILES + t


def rows_kernel(ga, gw, go, pa, pw, po, ar, wr, orr, ac, wc, oc, ta, to, packed, old_rows, old_cols, qa, qw, qo, sums, sems):
    copies = grad_copies((pa, pw, po), (qa, qw, qo), sems)
    for c in copies:
        c.start()
    old_rows[...] = jnp.zeros_like(old_rows)
    for which, k, t, at in row_places():
        old_rows[at : at + 1, :] = (ar, wr)[which][k : k + 1, t * LANES : (t + 1) * LANES]
    old_rows[R_WO:R_ALL, :] = orr[...]
    old_cols[...] = jnp.ones_like(old_cols)
    old_cols[0:A_MATS, :] = ac[...]
    for k, at, lo, hi in wi_places():
        old_cols[at : at + 1, 0 : hi - lo] = wc[k : k + 1, lo:hi]
    old_cols[C_WO : C_WO + 1, :] = oc[...]
    for k in range(A_MATS):
        for t in range(A_TILES):
            tile = slice(t * LANES, (t + 1) * LANES)
            g = ga[k, tile, :].T
            ta[k, tile, :] = g
            at = k * A_TILES + t
            packed[at : at + 1, :] = total(g * g + EPS_SQUARE)
    for t in range(O_TILES):
        tile = slice(t * LANES, (t + 1) * LANES)
        g = go[tile, :].T
        to[tile, :] = g
        packed[R_WO + t : R_WO + t + 1, :] = total(g * g + EPS_SQUARE)
    for k in range(W_MATS):
        for t in range(W_TILES):
            g = gw[k, :, t * LANES : (t + 1) * LANES]
            at = R_WI + k * W_TILES + t
            packed[at : at + 1, :] = total(g * g + EPS_SQUARE)
    sums[...] = jnp.zeros_like(sums)
    for k in range(A_MATS):
        copies[k].wait()
        p = qa[k]
        sums[k : k + 1, :] = total(p * p)
    for k in range(W_MATS):
        copies[A_MATS + k].wait()
        folded = jnp.zeros((W_COLS, LANES), jnp.float32)
        for t in range(W_TILES):
            p = qw[k, :, t * LANES : (t + 1) * LANES]
            folded = folded + p * p
        sums[A_MATS + k : A_MATS + k + 1, :] = total(folded)
    copies[-1].wait()
    p = qo[...]
    sums[N_MATS - 1 : N_MATS, :] = total(p * p)
    each = jnp.sum(sums[...], axis=1, keepdims=True)
    sub = lax.broadcasted_iota(jnp.int32, (8, LANES), 0)
    lane = lax.broadcasted_iota(jnp.int32, (8, LANES), 1)
    packed[R_ALL : R_ALL + 1, :] = total(jnp.where(sub == lane, each, 0.0))
    packed[R_ALL + 1 :, :] = jnp.zeros((packed.shape[0] - R_ALL - 1, LANES), jnp.float32)


def cols_kernel(got, old_cols, row_sums, ta, gw, to, send, cols, packed):
    tot = got[0]
    for n in range(1, got.shape[0]):
        tot = tot + got[n]
    at = lax.broadcasted_iota(jnp.int32, (C_ALL, LANES), 0)
    full_a, full_o = float(A_ROWS * got.shape[0]), float(O_ROWS * got.shape[0])
    mean = tot / jnp.where(at == C_WO, full_o, full_a)
    new = BETA * old_cols[...] + (1.0 - BETA) * mean
    cols[...] = new
    inv = 1.0 / new
    packed[0:R_ALL, :] = row_sums[0:R_ALL, :]
    packed[S_PARAM:S_ALL, :] = row_sums[R_ALL : R_ALL + S_ALL - S_PARAM, :]
    for k in range(A_MATS):
        weight = as_column(inv[k : k + 1, :])
        for t in range(A_TILES):
            at = R_ALL + k * A_TILES + t
            g = ta[k, t * LANES : (t + 1) * LANES, :]
            packed[at : at + 1, :] = total(g * g * weight)
    weight = as_column(inv[C_WO : C_WO + 1, :])
    for t in range(O_TILES):
        at = R_ALL + R_WO + t
        g = to[t * LANES : (t + 1) * LANES, :]
        packed[at : at + 1, :] = total(g * g * weight)
    for k in range(W_MATS):
        sums = [jnp.zeros((8, LANES), jnp.float32) for _ in range(W_TILES)]
        for b in range(W_COL_TILES):
            lo, hi = b * LANES, min((b + 1) * LANES, W_COLS)
            at = C_WI + k * W_COL_TILES + b
            weight = as_column(inv[at : at + 1, :])[0 : hi - lo, :]
            for t in range(W_TILES):
                g = gw[k, lo:hi, t * LANES : (t + 1) * LANES]
                part = (g * g * weight).reshape((hi - lo) // 8, 8, LANES)
                sums[t] = sums[t] + jnp.sum(part, axis=0)
        for t in range(W_TILES):
            at = R_ALL + R_WI + k * W_TILES + t
            packed[at : at + 1, :] = total(sums[t])
    value = packed[...]
    for n in range(send.shape[0]):
        send[n] = value


def relay_kernel(got, send):
    tot = got[0]
    for n in range(1, got.shape[0]):
        tot = tot + got[n]
    for n in range(send.shape[0]):
        send[n] = tot


def new_rows_kernel(n_col, got, old_rows, send, rows, tot, ratio):
    value = got[0]
    for n in range(1, got.shape[0]):
        value = value + got[n]
    tot[...] = value
    at = lax.broadcasted_iota(jnp.int32, (R_ALL, LANES), 0)
    full_a, full_w = float(LANES * n_col), float(W_COLS * n_col)
    full = jnp.where((at >= R_WI) & (at < R_WO), full_w, full_a)
    new = BETA * old_rows[0:R_ALL, :] + (1.0 - BETA) * (tot[0:R_ALL, :] / full)
    rows[0:R_ALL, :] = new
    rows[R_ALL:, :] = jnp.ones((rows.shape[0] - R_ALL, LANES), jnp.float32)
    ratio[...] = tot[R_ALL : 2 * R_ALL, :] / new
    spans = [(k * A_TILES, (k + 1) * A_TILES) for k in range(A_MATS)]
    spans += [(R_WI + k * W_TILES, R_WI + (k + 1) * W_TILES) for k in range(W_MATS)]
    spans += [(R_WO, R_ALL)]
    sub = lax.broadcasted_iota(jnp.int32, (8, LANES), 0)
    lane = lax.broadcasted_iota(jnp.int32, (8, LANES), 1)
    levels = jnp.zeros((8, LANES), jnp.float32)
    ratios = jnp.zeros((8, LANES), jnp.float32)
    for k, (lo, hi) in enumerate(spans):
        levels = jnp.where(sub == k, total(rows[lo:hi, :]), levels)
        ratios = jnp.where(sub == k, total(ratio[lo:hi, :]), ratios)
    params = jnp.where(sub == lane, tot[S_PARAM : S_PARAM + 1, :], 0.0)
    levels = jnp.sum(levels, axis=1, keepdims=True)
    ratios = jnp.sum(ratios, axis=1, keepdims=True)
    params = jnp.sum(params, axis=1, keepdims=True)
    value = jnp.where(lane < 32, levels, jnp.where(lane < 64, ratios, params))
    for n in range(send.shape[0]):
        send[n] = value


def scaled_kernel(ta, gw, to, rows, cols, ua, uw, uo, ar, wr, orr, ac, wc, oc):
    for which, k, t, at in row_places():
        (ar, wr)[which][k : k + 1, t * LANES : (t + 1) * LANES] = rows[at : at + 1, :]
    orr[...] = rows[R_WO:R_ALL, :]
    ac[...] = cols[0:A_MATS, :]
    for k, at, lo, hi in wi_places():
        wc[k : k + 1, lo:hi] = cols[at : at + 1, 0 : hi - lo]
    oc[...] = cols[C_WO : C_WO + 1, :]
    left = lax.rsqrt(rows[0:R_ALL, :])
    right = lax.rsqrt(cols[...])
    for k in range(A_MATS):
        column = as_column(right[k : k + 1, :])
        for t in range(A_TILES):
            at = k * A_TILES + t
            tile = slice(t * LANES, (t + 1) * LANES)
            ua[k, tile, :] = (ta[k, tile, :] * column * left[at : at + 1, :]).T
    column = as_column(right[C_WO : C_WO + 1, :])
    for t in range(O_TILES):
        at = R_WO + t
        tile = slice(t * LANES, (t + 1) * LANES)
        uo[tile, :] = (to[tile, :] * column * left[at : at + 1, :]).T
    for k, at, lo, hi in wi_places():
        column = as_column(right[at : at + 1, :])[0 : hi - lo, :]
        for t in range(W_TILES):
            row = R_WI + k * W_TILES + t
            tile = slice(t * LANES, (t + 1) * LANES)
            uw[k, lo:hi, tile] = gw[k, lo:hi, tile] * column * left[row : row + 1, :]


def update_kernel(n_col, got, ua, uw, uo, a, w, o, va, vw, vo, sems):
    tot = got[0]
    for n in range(1, got.shape[0]):
        tot = tot + got[n]
    sub = lax.broadcasted_iota(jnp.int32, (8, 1), 0)
    n_row = got.shape[0]
    full_rows = jnp.where(sub == N_MATS - 1, float(O_ROWS * n_row), float(A_ROWS * n_row))
    wide = (sub >= A_MATS) & (sub < A_MATS + W_MATS)
    full_cols = jnp.where(wide, float(W_COLS * n_col), float(LANES * n_col))
    count = full_rows * full_cols
    level = tot[:, 0:1] / full_rows
    dir_rms = jnp.sqrt(level * tot[:, 32:33] / count)
    param_rms = jnp.sqrt(tot[:, 64:65] / count)
    factor = -RHO * param_rms / jnp.maximum(1.0, dir_rms) * jnp.sqrt(level)
    copies = grad_copies((va, vw, vo), (a, w, o), sems)
    for k in range(A_MATS):
        va[k] = ua[k] * factor[k : k + 1, :]
        copies[k].start()
    for k in range(W_MATS):
        vw[k] = uw[k] * factor[A_MATS + k : A_MATS + k + 1, :]
        copies[A_MATS + k].start()
    vo[...] = uo[...] * factor[N_MATS - 1 : N_MATS, :]
    copies[-1].start()
    for c in copies:
        c.wait()


def exchange(x, axes):
    return lax.all_to_all(x, axes, 0, 0)


def shards(
    attn_grad,
    attn_param,
    attn_rows,
    attn_cols,
    wi_grad,
    wi_param,
    wi_rows,
    wi_cols,
    wo_grad,
    wo_param,
    wo_rows,
    wo_cols,
):
    n_row, n_near, n_far = (lax.axis_size(axes) for axes in (ROW, NEAR, FAR))
    n_col = n_near * n_far
    wi_grad = jnp.swapaxes(wi_grad, 1, 2)
    wi_param = jnp.swapaxes(wi_param, 1, 2)
    blocks = ((A_MATS, A_ROWS, LANES), (W_MATS, W_COLS, W_ROWS), (O_ROWS, LANES))
    held = [vmem(*b) for b in blocks]
    sems = pltpu.SemaphoreType.DMA((N_MATS,))
    send, ga, gw, go = call(
        load_kernel,
        [f32(n_row, C_ALL, LANES)] + held,
        [ANYWHERE] * 3,
        [WHOLE] * 4,
        [vmem(C_ALL, LANES), sems],
        bytes_accessed=3 << 20,
    )(far(attn_grad), far(wi_grad), far(wo_grad))
    got = exchange(send, ROW)
    ga, gw, go = here(ga), here(gw), here(go)
    ta, to, row_sums, old_rows, old_cols = call(
        rows_kernel,
        [held[0], held[2], vmem(40, LANES), vmem(40, LANES), vmem(C_ALL, LANES)],
        [WHOLE] * 3 + [ANYWHERE] * 3 + [WHOLE] * 6,
        [WHOLE] * 5,
        held + [vmem(8, LANES), sems],
        bytes_accessed=6 << 20,
        aliases={0: 0, 2: 1},
    )(
        ga,
        gw,
        go,
        far(attn_param),
        far(wi_param),
        far(wo_param),
        attn_rows,
        wi_rows,
        wo_rows.reshape(O_TILES, LANES),
        attn_cols,
        wi_cols,
        wo_cols.reshape(1, LANES),
    )
    ta, to = here(ta), here(to)
    send, cols = call(
        cols_kernel,
        [f32(n_near, S_ALL, LANES), vmem(C_ALL, LANES)],
        [WHOLE] * 6,
        [WHOLE] * 2,
        [vmem(S_ALL, LANES)],
        bytes_accessed=3 << 20,
    )(got, here(old_cols), here(row_sums), ta, gw, to)
    got = exchange(send, NEAR)
    send = call(relay_kernel, f32(n_far, S_ALL, LANES), [WHOLE], WHOLE)(got)
    got = exchange(send, FAR)
    send, rows = call(
        lambda *refs: new_rows_kernel(n_col, *refs),
        [f32(n_row, 8, LANES), vmem(40, LANES)],
        [WHOLE] * 2,
        [WHOLE] * 2,
        [vmem(S_ALL, LANES), vmem(R_ALL, LANES)],
    )(got, here(old_rows))
    got = exchange(send, ROW)
    ua, uw, uo, attn_rows_new, wi_rows_new, wo_rows_new, attn_cols_new, wi_cols_new, wo_cols_new = call(
        scaled_kernel,
        held
        + [
            f32(A_MATS, A_ROWS),
            f32(W_MATS, W_ROWS),
            f32(O_TILES, LANES),
            f32(A_MATS, LANES),
            f32(W_MATS, W_COLS),
            f32(1, LANES),
        ],
        [WHOLE] * 5,
        [WHOLE] * 9,
        bytes_accessed=6 << 20,
        aliases={0: 0, 1: 1, 2: 2},
    )(ta, gw, to, here(rows), here(cols))
    attn_update, wi_update, wo_update = call(
        lambda *refs: update_kernel(n_col, *refs),
        [hbm(*b) for b in blocks],
        [WHOLE] * 4,
        [ANYWHERE] * 3,
        held + [sems],
        bytes_accessed=3 << 20,
    )(got, here(ua), here(uw), here(uo))
    return (
        attn_update,
        attn_rows_new,
        attn_cols_new,
        jnp.swapaxes(wi_update, 1, 2),
        wi_rows_new,
        wi_cols_new,
        wo_update,
        wo_rows_new.reshape(O_ROWS),
        wo_cols_new.reshape(LANES),
    )


def solution(mesh):
    fine = Mesh(mesh.devices.reshape(4, 2, 4, 4, 2), ROW + COL)
    big, row, col = P(None, ROW, COL), P(None, ROW), P(None, COL)
    return jax.shard_map(
        shards,
        mesh=fine,
        in_specs=(big, big, row, col, big, big, row, col, P(ROW, COL), P(ROW, COL), P(ROW), P(COL)),
        out_specs=(big, row, col, big, row, col, P(ROW, COL), P(ROW), P(COL)),
        check_vma=False,
    )
```

```python
import jax
import jax.numpy as jnp
from jax import lax
from jax.experimental import pallas as pl
from jax.experimental.pallas import tpu as pltpu
from jax.sharding import Mesh, PartitionSpec as P

STEP = 2
EPS_SQUARE = 1e-30
BETA = 1.0 - STEP ** (-0.8)
RHO = STEP ** (-0.5)
LANES = 128
N_MATS = 7

ROW = ("y", "core")
COL = ("x", "zq", "zp")
NEAR = ("x", "zp")
FAR = ("zq",)

A_MATS, A_ROWS = 4, 512
W_MATS, W_COLS, W_ROWS = 2, 320, 512
O_ROWS = 1280
A_TILES, O_TILES, W_TILES = A_ROWS // LANES, O_ROWS // LANES, W_ROWS // LANES
W_COL_TILES = -(-W_COLS // LANES)

C_WI, C_WO, C_ALL = 4, 10, 16
R_WI, R_WO, R_ALL = 16, 24, 34
S_PARAM, S_ALL = 2 * R_ALL, 72

N_WRITES = 3 + 2 * W_MATS + (A_MATS * A_TILES + O_TILES) // 2

VMEM_LIMIT = 48 * 1024 * 1024
WHOLE = pl.BlockSpec(memory_space=pltpu.VMEM)
ANYWHERE = pl.BlockSpec(memory_space=pl.ANY)


def call(body, out_shape, in_specs, out_specs, scratch=(), bytes_accessed=1 << 20, aliases=None):
    return pl.pallas_call(
        body,
        out_shape=out_shape,
        in_specs=in_specs,
        out_specs=out_specs,
        scratch_shapes=list(scratch),
        input_output_aliases=aliases or {},
        compiler_params=pltpu.CompilerParams(vmem_limit_bytes=VMEM_LIMIT),
        cost_estimate=pl.CostEstimate(flops=4 << 20, bytes_accessed=bytes_accessed, transcendentals=0),
    )


def here(x):
    return pltpu.with_memory_space_constraint(x, pltpu.VMEM)


def far(x):
    return pltpu.with_memory_space_constraint(x, pltpu.HBM)


def f32(*shape):
    return jax.ShapeDtypeStruct(shape, jnp.float32)


def vmem(*shape):
    return pltpu.VMEM(shape, jnp.float32)


def hbm(*shape):
    return pltpu.HBM(shape, jnp.float32)


def grad_copies(sources, targets, sems):
    a, w, o = sources
    a_to, w_to, o_to = targets
    pairs = [(a.at[k], a_to.at[k]) for k in range(A_MATS)]
    pairs += [(w.at[k], w_to.at[k]) for k in range(W_MATS)]
    pairs += [(o, o_to)]
    return [pltpu.make_async_copy(s, t, sems.at[i]) for i, (s, t) in enumerate(pairs)]


def total(x):
    return jnp.sum(x, axis=0, keepdims=True)


def as_column(row):
    return jnp.broadcast_to(row, (LANES, LANES)).T


def load_kernel(a, w, o, send, ga, gw, go, packed, sems):
    copies = grad_copies((a, w, o), (ga, gw, go), sems)
    for c in copies:
        c.start()
    packed[...] = jnp.zeros_like(packed)
    for k in range(A_MATS):
        copies[k].wait()
        g = ga[k]
        packed[k : k + 1, :] = total(g * g + EPS_SQUARE)
    for k in range(W_MATS):
        copies[A_MATS + k].wait()
        for b in range(W_COL_TILES):
            lo, hi = b * LANES, min((b + 1) * LANES, W_COLS)
            folded = jnp.zeros((hi - lo, LANES), jnp.float32)
            for t in range(W_TILES):
                g = gw[k, lo:hi, t * LANES : (t + 1) * LANES]
                folded = folded + (g * g + EPS_SQUARE)
            if hi - lo < LANES:
                folded = jnp.concatenate([folded, jnp.zeros((LANES - hi + lo, LANES), jnp.float32)], axis=0)
            at = C_WI + k * W_COL_TILES + b
            packed[at : at + 1, :] = total(folded.T)
    copies[-1].wait()
    g = go[...]
    packed[C_WO : C_WO + 1, :] = total(g * g + EPS_SQUARE)
    value = packed[...]
    for n in range(send.shape[0]):
        send[n] = value


def wi_places():
    for k in range(W_MATS):
        for b in range(W_COL_TILES):
            lo, hi = b * LANES, min((b + 1) * LANES, W_COLS)
            yield k, C_WI + k * W_COL_TILES + b, lo, hi


def row_places():
    for k in range(A_MATS):
        for t in range(A_TILES):
            yield 0, k, t, k * A_TILES + t
    for k in range(W_MATS):
        for t in range(W_TILES):
            yield 1, k, t, R_WI + k * W_TILES + t


def rows_kernel(ga, gw, go, pa, pw, po, ar, wr, orr, ac, wc, oc, ta, to, packed, old_rows, old_cols, qa, qw, qo, sums, sems):
    copies = grad_copies((pa, pw, po), (qa, qw, qo), sems)
    for c in copies:
        c.start()
    old_rows[...] = jnp.zeros_like(old_rows)
    for which, k, t, at in row_places():
        old_rows[at : at + 1, :] = (ar, wr)[which][k : k + 1, t * LANES : (t + 1) * LANES]
    old_rows[R_WO:R_ALL, :] = orr[...]
    old_cols[...] = jnp.ones_like(old_cols)
    old_cols[0:A_MATS, :] = ac[...]
    for k, at, lo, hi in wi_places():
        old_cols[at : at + 1, 0 : hi - lo] = wc[k : k + 1, lo:hi]
    old_cols[C_WO : C_WO + 1, :] = oc[...]
    for k in range(A_MATS):
        for t in range(A_TILES):
            tile = slice(t * LANES, (t + 1) * LANES)
            g = ga[k, tile, :].T
            ta[k, tile, :] = g
            at = k * A_TILES + t
            packed[at : at + 1, :] = total(g * g + EPS_SQUARE)
    for t in range(O_TILES):
        tile = slice(t * LANES, (t + 1) * LANES)
        g = go[tile, :].T
        to[tile, :] = g
        packed[R_WO + t : R_WO + t + 1, :] = total(g * g + EPS_SQUARE)
    for k in range(W_MATS):
        for t in range(W_TILES):
            g = gw[k, :, t * LANES : (t + 1) * LANES]
            at = R_WI + k * W_TILES + t
            packed[at : at + 1, :] = total(g * g + EPS_SQUARE)
    sums[...] = jnp.zeros_like(sums)
    for k in range(A_MATS):
        copies[k].wait()
        p = qa[k]
        sums[k : k + 1, :] = total(p * p)
    for k in range(W_MATS):
        copies[A_MATS + k].wait()
        folded = jnp.zeros((W_COLS, LANES), jnp.float32)
        for t in range(W_TILES):
            p = qw[k, :, t * LANES : (t + 1) * LANES]
            folded = folded + p * p
        sums[A_MATS + k : A_MATS + k + 1, :] = total(folded)
    copies[-1].wait()
    p = qo[...]
    sums[N_MATS - 1 : N_MATS, :] = total(p * p)
    each = jnp.sum(sums[...], axis=1, keepdims=True)
    sub = lax.broadcasted_iota(jnp.int32, (8, LANES), 0)
    lane = lax.broadcasted_iota(jnp.int32, (8, LANES), 1)
    packed[R_ALL : R_ALL + 1, :] = total(jnp.where(sub == lane, each, 0.0))
    packed[R_ALL + 1 :, :] = jnp.zeros((packed.shape[0] - R_ALL - 1, LANES), jnp.float32)


def cols_kernel(got, old_cols, row_sums, ta, gw, to, send, cols, packed):
    tot = got[0]
    for n in range(1, got.shape[0]):
        tot = tot + got[n]
    at = lax.broadcasted_iota(jnp.int32, (C_ALL, LANES), 0)
    full_a, full_o = float(A_ROWS * got.shape[0]), float(O_ROWS * got.shape[0])
    mean = tot / jnp.where(at == C_WO, full_o, full_a)
    new = BETA * old_cols[...] + (1.0 - BETA) * mean
    cols[...] = new
    inv = 1.0 / new
    packed[0:R_ALL, :] = row_sums[0:R_ALL, :]
    packed[S_PARAM:S_ALL, :] = row_sums[R_ALL : R_ALL + S_ALL - S_PARAM, :]
    for k in range(A_MATS):
        weight = as_column(inv[k : k + 1, :])
        for t in range(A_TILES):
            at = R_ALL + k * A_TILES + t
            g = ta[k, t * LANES : (t + 1) * LANES, :]
            packed[at : at + 1, :] = total(g * g * weight)
    weight = as_column(inv[C_WO : C_WO + 1, :])
    for t in range(O_TILES):
        at = R_ALL + R_WO + t
        g = to[t * LANES : (t + 1) * LANES, :]
        packed[at : at + 1, :] = total(g * g * weight)
    for k in range(W_MATS):
        sums = [jnp.zeros((8, LANES), jnp.float32) for _ in range(W_TILES)]
        for b in range(W_COL_TILES):
            lo, hi = b * LANES, min((b + 1) * LANES, W_COLS)
            at = C_WI + k * W_COL_TILES + b
            weight = as_column(inv[at : at + 1, :])[0 : hi - lo, :]
            for t in range(W_TILES):
                g = gw[k, lo:hi, t * LANES : (t + 1) * LANES]
                part = (g * g * weight).reshape((hi - lo) // 8, 8, LANES)
                sums[t] = sums[t] + jnp.sum(part, axis=0)
        for t in range(W_TILES):
            at = R_ALL + R_WI + k * W_TILES + t
            packed[at : at + 1, :] = total(sums[t])
    value = packed[...]
    for n in range(send.shape[0]):
        send[n] = value


def relay_kernel(got, send):
    tot = got[0]
    for n in range(1, got.shape[0]):
        tot = tot + got[n]
    send[...] = tot


def new_rows_kernel(n_col, old_rows, done, own, before, after, opposite, send, rows, tot, ratio):
    tot[...] = (own[...] + opposite[...]) + (before[...] + after[...])
    at = lax.broadcasted_iota(jnp.int32, (R_ALL, LANES), 0)
    full_a, full_w = float(LANES * n_col), float(W_COLS * n_col)
    full = jnp.where((at >= R_WI) & (at < R_WO), full_w, full_a)
    new = BETA * old_rows[0:R_ALL, :] + (1.0 - BETA) * (tot[0:R_ALL, :] / full)
    rows[0:R_ALL, :] = new
    rows[R_ALL:, :] = jnp.ones((rows.shape[0] - R_ALL, LANES), jnp.float32)
    ratio[...] = tot[R_ALL : 2 * R_ALL, :] / new
    spans = [(k * A_TILES, (k + 1) * A_TILES) for k in range(A_MATS)]
    spans += [(R_WI + k * W_TILES, R_WI + (k + 1) * W_TILES) for k in range(W_MATS)]
    spans += [(R_WO, R_ALL)]
    sub = lax.broadcasted_iota(jnp.int32, (8, LANES), 0)
    lane = lax.broadcasted_iota(jnp.int32, (8, LANES), 1)
    levels = jnp.zeros((8, LANES), jnp.float32)
    ratios = jnp.zeros((8, LANES), jnp.float32)
    for k, (lo, hi) in enumerate(spans):
        levels = jnp.where(sub == k, total(rows[lo:hi, :]), levels)
        ratios = jnp.where(sub == k, total(ratio[lo:hi, :]), ratios)
    params = jnp.where(sub == lane, tot[S_PARAM : S_PARAM + 1, :], 0.0)
    levels = jnp.sum(levels, axis=1, keepdims=True)
    ratios = jnp.sum(ratios, axis=1, keepdims=True)
    params = jnp.sum(params, axis=1, keepdims=True)
    value = jnp.where(lane < 32, levels, jnp.where(lane < 64, ratios, params))
    for n in range(send.shape[0]):
        send[n] = value


def scaled_kernel(ta, gw, to, cols, after, ua, uw, uo, ac, wc, oc, done):
    done[...] = jnp.zeros_like(done)
    ac[...] = cols[0:A_MATS, :]
    for k, at, lo, hi in wi_places():
        wc[k : k + 1, lo:hi] = cols[at : at + 1, 0 : hi - lo]
    oc[...] = cols[C_WO : C_WO + 1, :]
    right = lax.rsqrt(cols[...])
    for k in range(A_MATS):
        column = as_column(right[k : k + 1, :])
        for t in range(A_TILES):
            tile = slice(t * LANES, (t + 1) * LANES)
            ua[k, tile, :] = ta[k, tile, :] * column
    column = as_column(right[C_WO : C_WO + 1, :])
    for t in range(O_TILES):
        tile = slice(t * LANES, (t + 1) * LANES)
        uo[tile, :] = to[tile, :] * column
    for k, at, lo, hi in wi_places():
        column = as_column(right[at : at + 1, :])[0 : hi - lo, :]
        for t in range(W_TILES):
            tile = slice(t * LANES, (t + 1) * LANES)
            uw[k, lo:hi, tile] = gw[k, lo:hi, tile] * column


def update_kernel(n_col, got, rows, ua, uw, uo, a, w, o, ar, wr, orr, va, vw, vo, var, vwr, sems):
    small = [(var, ar), (vwr, wr), (rows.at[R_WO:R_ALL, :], orr)]
    copies = [pltpu.make_async_copy(s, t, sems.at[i]) for i, (s, t) in enumerate(small)]
    for which, k, t, at in row_places():
        (var, vwr)[which][k : k + 1, t * LANES : (t + 1) * LANES] = rows[at : at + 1, :]
    for c in copies:
        c.start()

    def write(source, target):
        copies.append(pltpu.make_async_copy(source, target, sems.at[len(copies)]))
        copies[-1].start()

    left = lax.rsqrt(rows[0:R_ALL, :])
    tot = got[0]
    for n in range(1, got.shape[0]):
        tot = tot + got[n]
    sub = lax.broadcasted_iota(jnp.int32, (8, 1), 0)
    n_row = got.shape[0]
    full_rows = jnp.where(sub == N_MATS - 1, float(O_ROWS * n_row), float(A_ROWS * n_row))
    wide = (sub >= A_MATS) & (sub < A_MATS + W_MATS)
    full_cols = jnp.where(wide, float(W_COLS * n_col), float(LANES * n_col))
    count = full_rows * full_cols
    level = tot[:, 0:1] / full_rows
    dir_rms = jnp.sqrt(level * tot[:, 32:33] / count)
    param_rms = jnp.sqrt(tot[:, 64:65] / count)
    factor = -RHO * param_rms / jnp.maximum(1.0, dir_rms) * jnp.sqrt(level)
    for k in range(W_MATS):
        f = factor[A_MATS + k : A_MATS + k + 1, :]
        scale = [left[R_WI + k * W_TILES + t : R_WI + k * W_TILES + t + 1, :] * f for t in range(W_TILES)]
        for lo, hi in ((0, W_COLS // 2), (W_COLS // 2, W_COLS)):
            for t in range(W_TILES):
                tile = slice(t * LANES, (t + 1) * LANES)
                vw[k, lo:hi, tile] = uw[k, lo:hi, tile] * scale[t]
            write(vw.at[k, lo:hi], w.at[k, lo:hi])
    for k in range(A_MATS):
        f = factor[k : k + 1, :]
        for t in range(A_TILES):
            at = k * A_TILES + t
            tile = slice(t * LANES, (t + 1) * LANES)
            va[k, tile, :] = (ua[k, tile, :] * (left[at : at + 1, :] * f)).T
            if t % 2:
                half = slice((t - 1) * LANES, (t + 1) * LANES)
                write(va.at[k, half], a.at[k, half])
    f = factor[N_MATS - 1 : N_MATS, :]
    for t in range(O_TILES):
        at = R_WO + t
        tile = slice(t * LANES, (t + 1) * LANES)
        vo[tile, :] = (uo[tile, :] * (left[at : at + 1, :] * f)).T
        if t % 2:
            half = slice((t - 1) * LANES, (t + 1) * LANES)
            write(vo.at[half], o.at[half])
    for c in copies:
        c.wait()


def exchange(x, axes):
    return lax.all_to_all(x, axes, 0, 0)


def quad(x, axis, order):
    got = {0: x}
    for shift in order:
        got[shift] = lax.ppermute(x, axis, [(i, (i + shift) % 4) for i in range(4)])
    return [got[shift] for shift in (0, 1, 3, 2)]


def shards(
    attn_grad,
    attn_param,
    attn_rows,
    attn_cols,
    wi_grad,
    wi_param,
    wi_rows,
    wi_cols,
    wo_grad,
    wo_param,
    wo_rows,
    wo_cols,
):
    n_row, n_near, n_far = (lax.axis_size(axes) for axes in (ROW, NEAR, FAR))
    n_col = n_near * n_far
    wi_grad = jnp.swapaxes(wi_grad, 1, 2)
    wi_param = jnp.swapaxes(wi_param, 1, 2)
    blocks = ((A_MATS, A_ROWS, LANES), (W_MATS, W_COLS, W_ROWS), (O_ROWS, LANES))
    held = [vmem(*b) for b in blocks]
    sems = pltpu.SemaphoreType.DMA((N_MATS,))
    send, ga, gw, go = call(
        load_kernel,
        [f32(n_row, C_ALL, LANES)] + held,
        [ANYWHERE] * 3,
        [WHOLE] * 4,
        [vmem(C_ALL, LANES), sems],
        bytes_accessed=3 << 20,
    )(far(attn_grad), far(wi_grad), far(wo_grad))
    got = exchange(send, ROW)
    ga, gw, go = here(ga), here(gw), here(go)
    ta, to, row_sums, old_rows, old_cols = call(
        rows_kernel,
        [held[0], held[2], vmem(40, LANES), vmem(40, LANES), vmem(C_ALL, LANES)],
        [WHOLE] * 3 + [ANYWHERE] * 3 + [WHOLE] * 6,
        [WHOLE] * 5,
        held + [vmem(8, LANES), sems],
        bytes_accessed=6 << 20,
        aliases={0: 0, 2: 1},
    )(
        ga,
        gw,
        go,
        far(attn_param),
        far(wi_param),
        far(wo_param),
        attn_rows,
        wi_rows,
        wo_rows.reshape(O_TILES, LANES),
        attn_cols,
        wi_cols,
        wo_cols.reshape(1, LANES),
    )
    ta, to = here(ta), here(to)
    send, cols = call(
        cols_kernel,
        [f32(n_near, S_ALL, LANES), vmem(C_ALL, LANES)],
        [WHOLE] * 6,
        [WHOLE] * 2,
        [vmem(S_ALL, LANES)],
        bytes_accessed=3 << 20,
    )(got, here(old_cols), here(row_sums), ta, gw, to)
    got = exchange(send, NEAR)
    send = call(relay_kernel, f32(S_ALL, LANES), [WHOLE], WHOLE)(got)
    got = quad(send, "zq", (1, 3, 2))
    ua, uw, uo, attn_cols_new, wi_cols_new, wo_cols_new, done = call(
        scaled_kernel,
        held + [f32(A_MATS, LANES), f32(W_MATS, W_COLS), f32(1, LANES), vmem(8, LANES)],
        [WHOLE] * 4 + [ANYWHERE],
        [WHOLE] * 7,
        bytes_accessed=6 << 20,
        aliases={0: 0, 1: 1, 2: 2},
    )(ta, gw, to, here(cols), send)
    send, rows = call(
        lambda *refs: new_rows_kernel(n_col, *refs),
        [f32(n_row, 8, LANES), vmem(40, LANES)],
        [WHOLE, ANYWHERE] + [WHOLE] * 4,
        [WHOLE] * 2,
        [vmem(S_ALL, LANES), vmem(R_ALL, LANES)],
    )(here(old_rows), here(done), *got)
    got = exchange(send, ROW)
    attn_update, wi_update, wo_update, attn_rows_new, wi_rows_new, wo_rows_new = call(
        lambda *refs: update_kernel(n_col, *refs),
        [hbm(*b) for b in blocks] + [hbm(A_MATS, A_ROWS), hbm(W_MATS, W_ROWS), hbm(O_TILES, LANES)],
        [WHOLE] * 5,
        [ANYWHERE] * 6,
        held + [vmem(A_MATS, A_ROWS), vmem(W_MATS, W_ROWS), pltpu.SemaphoreType.DMA((N_WRITES,))],
        bytes_accessed=3 << 20,
    )(got, here(rows), here(ua), here(uw), here(uo))
    return (
        attn_update,
        attn_rows_new,
        attn_cols_new,
        jnp.swapaxes(wi_update, 1, 2),
        wi_rows_new,
        wi_cols_new,
        wo_update,
        wo_rows_new.reshape(O_ROWS),
        wo_cols_new.reshape(LANES),
    )


def solution(mesh):
    fine = Mesh(mesh.devices.reshape(4, 2, 4, 4, 2), ROW + COL)
    big, row, col = P(None, ROW, COL), P(None, ROW), P(None, COL)
    return jax.shard_map(
        shards,
        mesh=fine,
        in_specs=(big, big, row, col, big, big, row, col, P(ROW, COL), P(ROW, COL), P(ROW), P(COL)),
        out_specs=(big, row, col, big, row, col, P(ROW, COL), P(ROW), P(COL)),
        check_vma=False,
    )
```

```python
import jax
import jax.numpy as jnp
from jax import lax
from jax.experimental import pallas as pl
from jax.experimental.pallas import tpu as pltpu
from jax.sharding import Mesh, PartitionSpec as P

STEP = 2
EPS_SQUARE = 1e-30
BETA = 1.0 - STEP ** (-0.8)
RHO = STEP ** (-0.5)
LANES = 128
N_MATS = 7

ROW = ("y", "core")
COL = ("x", "z")

A_MATS, A_ROWS = 4, 512
W_MATS, W_COLS, W_ROWS = 2, 320, 512
O_ROWS = 1280
A_TILES, O_TILES, W_TILES = A_ROWS // LANES, O_ROWS // LANES, W_ROWS // LANES
W_COL_TILES = -(-W_COLS // LANES)

C_WI, C_WO, C_ALL = 4, 10, 16
R_WI, R_WO, R_ALL = 16, 24, 34
S_PARAM, S_ALL = 2 * R_ALL, 72

N_WRITES = 3 + 2 * W_MATS + (A_MATS * A_TILES + O_TILES) // 2

VMEM_LIMIT = 48 * 1024 * 1024
WHOLE = pl.BlockSpec(memory_space=pltpu.VMEM)
ANYWHERE = pl.BlockSpec(memory_space=pl.ANY)


def call(body, out_shape, in_specs, out_specs, scratch=(), bytes_accessed=1 << 20, aliases=None):
    return pl.pallas_call(
        body,
        out_shape=out_shape,
        in_specs=in_specs,
        out_specs=out_specs,
        scratch_shapes=list(scratch),
        input_output_aliases=aliases or {},
        compiler_params=pltpu.CompilerParams(vmem_limit_bytes=VMEM_LIMIT),
        cost_estimate=pl.CostEstimate(flops=4 << 20, bytes_accessed=bytes_accessed, transcendentals=0),
    )


def here(x):
    return pltpu.with_memory_space_constraint(x, pltpu.VMEM)


def far(x):
    return pltpu.with_memory_space_constraint(x, pltpu.HBM)


def f32(*shape):
    return jax.ShapeDtypeStruct(shape, jnp.float32)


def vmem(*shape):
    return pltpu.VMEM(shape, jnp.float32)


def hbm(*shape):
    return pltpu.HBM(shape, jnp.float32)


def grad_copies(sources, targets, sems):
    a, w, o = sources
    a_to, w_to, o_to = targets
    pairs = [(a.at[k], a_to.at[k]) for k in range(A_MATS)]
    pairs += [(w.at[k], w_to.at[k]) for k in range(W_MATS)]
    pairs += [(o, o_to)]
    return [pltpu.make_async_copy(s, t, sems.at[i]) for i, (s, t) in enumerate(pairs)]


def total(x):
    return jnp.sum(x, axis=0, keepdims=True)


def as_column(row):
    return jnp.broadcast_to(row, (LANES, LANES)).T


def load_kernel(a, w, o, send, ga, gw, go, packed, sems):
    copies = grad_copies((a, w, o), (ga, gw, go), sems)
    for c in copies:
        c.start()
    packed[...] = jnp.zeros_like(packed)
    for k in range(A_MATS):
        copies[k].wait()
        g = ga[k]
        packed[k : k + 1, :] = total(g * g + EPS_SQUARE)
    for k in range(W_MATS):
        copies[A_MATS + k].wait()
        for b in range(W_COL_TILES):
            lo, hi = b * LANES, min((b + 1) * LANES, W_COLS)
            folded = jnp.zeros((hi - lo, LANES), jnp.float32)
            for t in range(W_TILES):
                g = gw[k, lo:hi, t * LANES : (t + 1) * LANES]
                folded = folded + (g * g + EPS_SQUARE)
            if hi - lo < LANES:
                folded = jnp.concatenate([folded, jnp.zeros((LANES - hi + lo, LANES), jnp.float32)], axis=0)
            at = C_WI + k * W_COL_TILES + b
            packed[at : at + 1, :] = total(folded.T)
    copies[-1].wait()
    g = go[...]
    packed[C_WO : C_WO + 1, :] = total(g * g + EPS_SQUARE)
    value = packed[...]
    for n in range(send.shape[0]):
        send[n] = value


def wi_places():
    for k in range(W_MATS):
        for b in range(W_COL_TILES):
            lo, hi = b * LANES, min((b + 1) * LANES, W_COLS)
            yield k, C_WI + k * W_COL_TILES + b, lo, hi


def row_places():
    for k in range(A_MATS):
        for t in range(A_TILES):
            yield 0, k, t, k * A_TILES + t
    for k in range(W_MATS):
        for t in range(W_TILES):
            yield 1, k, t, R_WI + k * W_TILES + t


def rows_kernel(ga, gw, go, pa, pw, po, ar, wr, orr, ac, wc, oc, ta, to, packed, old_rows, old_cols, qa, qw, qo, sums, sems):
    copies = grad_copies((pa, pw, po), (qa, qw, qo), sems)
    for c in copies:
        c.start()
    old_rows[...] = jnp.zeros_like(old_rows)
    for which, k, t, at in row_places():
        old_rows[at : at + 1, :] = (ar, wr)[which][k : k + 1, t * LANES : (t + 1) * LANES]
    old_rows[R_WO:R_ALL, :] = orr[...]
    old_cols[...] = jnp.ones_like(old_cols)
    old_cols[0:A_MATS, :] = ac[...]
    for k, at, lo, hi in wi_places():
        old_cols[at : at + 1, 0 : hi - lo] = wc[k : k + 1, lo:hi]
    old_cols[C_WO : C_WO + 1, :] = oc[...]
    for k in range(A_MATS):
        for t in range(A_TILES):
            tile = slice(t * LANES, (t + 1) * LANES)
            g = ga[k, tile, :].T
            ta[k, tile, :] = g
            at = k * A_TILES + t
            packed[at : at + 1, :] = total(g * g + EPS_SQUARE)
    for t in range(O_TILES):
        tile = slice(t * LANES, (t + 1) * LANES)
        g = go[tile, :].T
        to[tile, :] = g
        packed[R_WO + t : R_WO + t + 1, :] = total(g * g + EPS_SQUARE)
    for k in range(W_MATS):
        for t in range(W_TILES):
            g = gw[k, :, t * LANES : (t + 1) * LANES]
            at = R_WI + k * W_TILES + t
            packed[at : at + 1, :] = total(g * g + EPS_SQUARE)
    sums[...] = jnp.zeros_like(sums)
    for k in range(A_MATS):
        copies[k].wait()
        p = qa[k]
        sums[k : k + 1, :] = total(p * p)
    for k in range(W_MATS):
        copies[A_MATS + k].wait()
        folded = jnp.zeros((W_COLS, LANES), jnp.float32)
        for t in range(W_TILES):
            p = qw[k, :, t * LANES : (t + 1) * LANES]
            folded = folded + p * p
        sums[A_MATS + k : A_MATS + k + 1, :] = total(folded)
    copies[-1].wait()
    p = qo[...]
    sums[N_MATS - 1 : N_MATS, :] = total(p * p)
    each = jnp.sum(sums[...], axis=1, keepdims=True)
    sub = lax.broadcasted_iota(jnp.int32, (8, LANES), 0)
    lane = lax.broadcasted_iota(jnp.int32, (8, LANES), 1)
    packed[R_ALL : R_ALL + 1, :] = total(jnp.where(sub == lane, each, 0.0))
    packed[R_ALL + 1 :, :] = jnp.zeros((packed.shape[0] - R_ALL - 1, LANES), jnp.float32)


def cols_kernel(got, old_cols, row_sums, ta, gw, to, send, cols, packed):
    tot = got[0]
    for n in range(1, got.shape[0]):
        tot = tot + got[n]
    at = lax.broadcasted_iota(jnp.int32, (C_ALL, LANES), 0)
    full_a, full_o = float(A_ROWS * got.shape[0]), float(O_ROWS * got.shape[0])
    mean = tot / jnp.where(at == C_WO, full_o, full_a)
    new = BETA * old_cols[...] + (1.0 - BETA) * mean
    cols[...] = new
    inv = 1.0 / new
    packed[0:R_ALL, :] = row_sums[0:R_ALL, :]
    packed[S_PARAM:S_ALL, :] = row_sums[R_ALL : R_ALL + S_ALL - S_PARAM, :]
    for k in range(A_MATS):
        weight = as_column(inv[k : k + 1, :])
        for t in range(A_TILES):
            at = R_ALL + k * A_TILES + t
            g = ta[k, t * LANES : (t + 1) * LANES, :]
            packed[at : at + 1, :] = total(g * g * weight)
    weight = as_column(inv[C_WO : C_WO + 1, :])
    for t in range(O_TILES):
        at = R_ALL + R_WO + t
        g = to[t * LANES : (t + 1) * LANES, :]
        packed[at : at + 1, :] = total(g * g * weight)
    for k in range(W_MATS):
        sums = [jnp.zeros((8, LANES), jnp.float32) for _ in range(W_TILES)]
        for b in range(W_COL_TILES):
            lo, hi = b * LANES, min((b + 1) * LANES, W_COLS)
            at = C_WI + k * W_COL_TILES + b
            weight = as_column(inv[at : at + 1, :])[0 : hi - lo, :]
            for t in range(W_TILES):
                g = gw[k, lo:hi, t * LANES : (t + 1) * LANES]
                part = (g * g * weight).reshape((hi - lo) // 8, 8, LANES)
                sums[t] = sums[t] + jnp.sum(part, axis=0)
        for t in range(W_TILES):
            at = R_ALL + R_WI + k * W_TILES + t
            packed[at : at + 1, :] = total(sums[t])
    send[...] = packed[...]


def sum4_kernel(own, beside, across, opposite, send):
    send[...] = (own[...] + opposite[...]) + (across[...] + beside[...])


def sum4_and_kernel(done, *refs):
    sum4_kernel(*refs)


def new_rows_kernel(n_col, old_rows, own, other, send, rows, tot, ratio):
    tot[...] = own[...] + other[...]
    at = lax.broadcasted_iota(jnp.int32, (R_ALL, LANES), 0)
    full_a, full_w = float(LANES * n_col), float(W_COLS * n_col)
    full = jnp.where((at >= R_WI) & (at < R_WO), full_w, full_a)
    new = BETA * old_rows[0:R_ALL, :] + (1.0 - BETA) * (tot[0:R_ALL, :] / full)
    rows[0:R_ALL, :] = new
    rows[R_ALL:, :] = jnp.ones((rows.shape[0] - R_ALL, LANES), jnp.float32)
    ratio[...] = tot[R_ALL : 2 * R_ALL, :] / new
    spans = [(k * A_TILES, (k + 1) * A_TILES) for k in range(A_MATS)]
    spans += [(R_WI + k * W_TILES, R_WI + (k + 1) * W_TILES) for k in range(W_MATS)]
    spans += [(R_WO, R_ALL)]
    sub = lax.broadcasted_iota(jnp.int32, (8, LANES), 0)
    lane = lax.broadcasted_iota(jnp.int32, (8, LANES), 1)
    levels = jnp.zeros((8, LANES), jnp.float32)
    ratios = jnp.zeros((8, LANES), jnp.float32)
    for k, (lo, hi) in enumerate(spans):
        levels = jnp.where(sub == k, total(rows[lo:hi, :]), levels)
        ratios = jnp.where(sub == k, total(ratio[lo:hi, :]), ratios)
    params = jnp.where(sub == lane, tot[S_PARAM : S_PARAM + 1, :], 0.0)
    levels = jnp.sum(levels, axis=1, keepdims=True)
    ratios = jnp.sum(ratios, axis=1, keepdims=True)
    params = jnp.sum(params, axis=1, keepdims=True)
    value = jnp.where(lane < 32, levels, jnp.where(lane < 64, ratios, params))
    for n in range(send.shape[0]):
        send[n] = value


def scaled_kernel(ta, gw, to, cols, after, ua, uw, uo, ac, wc, oc, done):
    done[...] = jnp.zeros_like(done)
    ac[...] = cols[0:A_MATS, :]
    for k, at, lo, hi in wi_places():
        wc[k : k + 1, lo:hi] = cols[at : at + 1, 0 : hi - lo]
    oc[...] = cols[C_WO : C_WO + 1, :]
    right = lax.rsqrt(cols[...])
    for k in range(A_MATS):
        column = as_column(right[k : k + 1, :])
        for t in range(A_TILES):
            tile = slice(t * LANES, (t + 1) * LANES)
            ua[k, tile, :] = ta[k, tile, :] * column
    column = as_column(right[C_WO : C_WO + 1, :])
    for t in range(O_TILES):
        tile = slice(t * LANES, (t + 1) * LANES)
        uo[tile, :] = to[tile, :] * column
    for k, at, lo, hi in wi_places():
        column = as_column(right[at : at + 1, :])[0 : hi - lo, :]
        for t in range(W_TILES):
            tile = slice(t * LANES, (t + 1) * LANES)
            uw[k, lo:hi, tile] = gw[k, lo:hi, tile] * column


def update_kernel(n_col, got, rows, ua, uw, uo, a, w, o, ar, wr, orr, va, vw, vo, var, vwr, sems):
    small = [(var, ar), (vwr, wr), (rows.at[R_WO:R_ALL, :], orr)]
    copies = [pltpu.make_async_copy(s, t, sems.at[i]) for i, (s, t) in enumerate(small)]
    for which, k, t, at in row_places():
        (var, vwr)[which][k : k + 1, t * LANES : (t + 1) * LANES] = rows[at : at + 1, :]
    for c in copies:
        c.start()

    def write(source, target):
        copies.append(pltpu.make_async_copy(source, target, sems.at[len(copies)]))
        copies[-1].start()

    left = lax.rsqrt(rows[0:R_ALL, :])
    tot = got[0]
    for n in range(1, got.shape[0]):
        tot = tot + got[n]
    sub = lax.broadcasted_iota(jnp.int32, (8, 1), 0)
    n_row = got.shape[0]
    full_rows = jnp.where(sub == N_MATS - 1, float(O_ROWS * n_row), float(A_ROWS * n_row))
    wide = (sub >= A_MATS) & (sub < A_MATS + W_MATS)
    full_cols = jnp.where(wide, float(W_COLS * n_col), float(LANES * n_col))
    count = full_rows * full_cols
    level = tot[:, 0:1] / full_rows
    dir_rms = jnp.sqrt(level * tot[:, 32:33] / count)
    param_rms = jnp.sqrt(tot[:, 64:65] / count)
    factor = -RHO * param_rms / jnp.maximum(1.0, dir_rms) * jnp.sqrt(level)
    for k in range(W_MATS):
        f = factor[A_MATS + k : A_MATS + k + 1, :]
        scale = [left[R_WI + k * W_TILES + t : R_WI + k * W_TILES + t + 1, :] * f for t in range(W_TILES)]
        for lo, hi in ((0, W_COLS // 2), (W_COLS // 2, W_COLS)):
            for t in range(W_TILES):
                tile = slice(t * LANES, (t + 1) * LANES)
                vw[k, lo:hi, tile] = uw[k, lo:hi, tile] * scale[t]
            write(vw.at[k, lo:hi], w.at[k, lo:hi])
    for k in range(A_MATS):
        f = factor[k : k + 1, :]
        for t in range(A_TILES):
            at = k * A_TILES + t
            tile = slice(t * LANES, (t + 1) * LANES)
            va[k, tile, :] = (ua[k, tile, :] * (left[at : at + 1, :] * f)).T
            if t % 2:
                half = slice((t - 1) * LANES, (t + 1) * LANES)
                write(va.at[k, half], a.at[k, half])
    f = factor[N_MATS - 1 : N_MATS, :]
    for t in range(O_TILES):
        at = R_WO + t
        tile = slice(t * LANES, (t + 1) * LANES)
        vo[tile, :] = (uo[tile, :] * (left[at : at + 1, :] * f)).T
        if t % 2:
            half = slice((t - 1) * LANES, (t + 1) * LANES)
            write(vo.at[half], o.at[half])
    for c in copies:
        c.wait()


def exchange(x, axes):
    return lax.all_to_all(x, axes, 0, 0)


PAIRINGS = (2, 3, 1)


def quad(x, axis):
    indices = range(lax.axis_size(axis))
    got = [lax.ppermute(x, axis, [(i, i ^ bits) for i in indices]) for bits in PAIRINGS]
    return [x] + got[::-1]


def mirror(x, axis):
    n = lax.axis_size(axis)
    return lax.ppermute(x, axis, [(i, n - 1 - i) for i in range(n)])


def shards(
    attn_grad,
    attn_param,
    attn_rows,
    attn_cols,
    wi_grad,
    wi_param,
    wi_rows,
    wi_cols,
    wo_grad,
    wo_param,
    wo_rows,
    wo_cols,
):
    n_row, n_col = lax.axis_size(ROW), lax.axis_size(COL)
    wi_grad = jnp.swapaxes(wi_grad, 1, 2)
    wi_param = jnp.swapaxes(wi_param, 1, 2)
    blocks = ((A_MATS, A_ROWS, LANES), (W_MATS, W_COLS, W_ROWS), (O_ROWS, LANES))
    held = [vmem(*b) for b in blocks]
    sems = pltpu.SemaphoreType.DMA((N_MATS,))
    send, ga, gw, go = call(
        load_kernel,
        [f32(n_row, C_ALL, LANES)] + held,
        [ANYWHERE] * 3,
        [WHOLE] * 4,
        [vmem(C_ALL, LANES), sems],
        bytes_accessed=3 << 20,
    )(far(attn_grad), far(wi_grad), far(wo_grad))
    got = exchange(send, ROW)
    ga, gw, go = here(ga), here(gw), here(go)
    ta, to, row_sums, old_rows, old_cols = call(
        rows_kernel,
        [held[0], held[2], vmem(40, LANES), vmem(40, LANES), vmem(C_ALL, LANES)],
        [WHOLE] * 3 + [ANYWHERE] * 3 + [WHOLE] * 6,
        [WHOLE] * 5,
        held + [vmem(8, LANES), sems],
        bytes_accessed=6 << 20,
        aliases={0: 0, 2: 1},
    )(
        ga,
        gw,
        go,
        far(attn_param),
        far(wi_param),
        far(wo_param),
        attn_rows,
        wi_rows,
        wo_rows.reshape(O_TILES, LANES),
        attn_cols,
        wi_cols,
        wo_cols.reshape(1, LANES),
    )
    ta, to = here(ta), here(to)
    send, cols = call(
        cols_kernel,
        [f32(S_ALL, LANES), vmem(C_ALL, LANES)],
        [WHOLE] * 6,
        [WHOLE] * 2,
        [vmem(S_ALL, LANES)],
        bytes_accessed=3 << 20,
    )(got, here(old_cols), here(row_sums), ta, gw, to)
    got = quad(send, "x")
    send = call(sum4_kernel, f32(S_ALL, LANES), [WHOLE] * 4, WHOLE)(*got)
    got = quad(send, "z")
    ua, uw, uo, attn_cols_new, wi_cols_new, wo_cols_new, done = call(
        scaled_kernel,
        held + [f32(A_MATS, LANES), f32(W_MATS, W_COLS), f32(1, LANES), vmem(8, LANES)],
        [WHOLE] * 4 + [ANYWHERE],
        [WHOLE] * 7,
        bytes_accessed=6 << 20,
        aliases={0: 0, 1: 1, 2: 2},
    )(ta, gw, to, here(cols), send)
    send = call(sum4_and_kernel, f32(S_ALL, LANES), [ANYWHERE] + [WHOLE] * 4, WHOLE)(here(done), *got)
    got = mirror(send, "z")
    send, rows = call(
        lambda *refs: new_rows_kernel(n_col, *refs),
        [f32(n_row, 8, LANES), vmem(40, LANES)],
        [WHOLE] * 3,
        [WHOLE] * 2,
        [vmem(S_ALL, LANES), vmem(R_ALL, LANES)],
    )(here(old_rows), send, got)
    got = exchange(send, ROW)
    attn_update, wi_update, wo_update, attn_rows_new, wi_rows_new, wo_rows_new = call(
        lambda *refs: update_kernel(n_col, *refs),
        [hbm(*b) for b in blocks] + [hbm(A_MATS, A_ROWS), hbm(W_MATS, W_ROWS), hbm(O_TILES, LANES)],
        [WHOLE] * 5,
        [ANYWHERE] * 6,
        held + [vmem(A_MATS, A_ROWS), vmem(W_MATS, W_ROWS), pltpu.SemaphoreType.DMA((N_WRITES,))],
        bytes_accessed=3 << 20,
    )(got, here(rows), here(ua), here(uw), here(uo))
    return (
        attn_update,
        attn_rows_new,
        attn_cols_new,
        jnp.swapaxes(wi_update, 1, 2),
        wi_rows_new,
        wi_cols_new,
        wo_update,
        wo_rows_new.reshape(O_ROWS),
        wo_cols_new.reshape(LANES),
    )


def solution(mesh):
    fine = Mesh(mesh.devices.reshape(4, 2, 4, 8), ROW + COL)
    big, row, col = P(None, ROW, COL), P(None, ROW), P(None, COL)
    return jax.shard_map(
        shards,
        mesh=fine,
        in_specs=(big, big, row, col, big, big, row, col, P(ROW, COL), P(ROW, COL), P(ROW), P(COL)),
        out_specs=(big, row, col, big, row, col, P(ROW, COL), P(ROW), P(COL)),
        check_vma=False,
    )
```

```python
import jax
import jax.numpy as jnp
from jax import lax
from jax.experimental import pallas as pl
from jax.experimental.pallas import tpu as pltpu
from jax.sharding import Mesh, PartitionSpec as P

STEP = 2
EPS_SQUARE = 1e-30
BETA = 1.0 - STEP ** (-0.8)
RHO = STEP ** (-0.5)
LANES = 128
N_MATS = 7

ROW = ("y", "core")
COL = ("x", "z")

A_MATS, A_ROWS = 4, 512
W_MATS, W_COLS, W_ROWS = 2, 320, 512
O_ROWS = 1280
A_TILES, O_TILES, W_TILES = A_ROWS // LANES, O_ROWS // LANES, W_ROWS // LANES
W_COL_TILES = -(-W_COLS // LANES)

C_WI, C_WO, C_ALL = 4, 10, 16
R_WI, R_WO, R_ALL = 16, 24, 34
S_PARAM, S_ALL = 2 * R_ALL, 72

N_WRITES = 3 + 2 * W_MATS + (A_MATS * A_TILES + O_TILES) // 2

VMEM_LIMIT = 48 * 1024 * 1024
WHOLE = pl.BlockSpec(memory_space=pltpu.VMEM)
ANYWHERE = pl.BlockSpec(memory_space=pl.ANY)


def call(body, out_shape, in_specs, out_specs, scratch=(), bytes_accessed=1 << 20, aliases=None):
    return pl.pallas_call(
        body,
        out_shape=out_shape,
        in_specs=in_specs,
        out_specs=out_specs,
        scratch_shapes=list(scratch),
        input_output_aliases=aliases or {},
        compiler_params=pltpu.CompilerParams(vmem_limit_bytes=VMEM_LIMIT),
        cost_estimate=pl.CostEstimate(flops=4 << 20, bytes_accessed=bytes_accessed, transcendentals=0),
    )


def here(x):
    return pltpu.with_memory_space_constraint(x, pltpu.VMEM)


def far(x):
    return pltpu.with_memory_space_constraint(x, pltpu.HBM)


def f32(*shape):
    return jax.ShapeDtypeStruct(shape, jnp.float32)


def vmem(*shape):
    return pltpu.VMEM(shape, jnp.float32)


def hbm(*shape):
    return pltpu.HBM(shape, jnp.float32)


def grad_copies(sources, targets, sems):
    a, w, o = sources
    a_to, w_to, o_to = targets
    pairs = [(a.at[k], a_to.at[k]) for k in range(A_MATS)]
    pairs += [(w.at[k], w_to.at[k]) for k in range(W_MATS)]
    pairs += [(o, o_to)]
    return [pltpu.make_async_copy(s, t, sems.at[i]) for i, (s, t) in enumerate(pairs)]


def total(x):
    return jnp.sum(x, axis=0, keepdims=True)


def as_column(row):
    return jnp.broadcast_to(row, (LANES, LANES)).T


def load_kernel(a, w, o, send, ga, gw, go, packed, sems):
    copies = grad_copies((a, w, o), (ga, gw, go), sems)
    for c in copies:
        c.start()
    packed[...] = jnp.zeros_like(packed)
    for k in range(A_MATS):
        copies[k].wait()
        g = ga[k]
        packed[k : k + 1, :] = total(g * g + EPS_SQUARE)
    for k in range(W_MATS):
        copies[A_MATS + k].wait()
        for b in range(W_COL_TILES):
            lo, hi = b * LANES, min((b + 1) * LANES, W_COLS)
            folded = jnp.zeros((hi - lo, LANES), jnp.float32)
            for t in range(W_TILES):
                g = gw[k, lo:hi, t * LANES : (t + 1) * LANES]
                folded = folded + (g * g + EPS_SQUARE)
            if hi - lo < LANES:
                folded = jnp.concatenate([folded, jnp.zeros((LANES - hi + lo, LANES), jnp.float32)], axis=0)
            at = C_WI + k * W_COL_TILES + b
            packed[at : at + 1, :] = total(folded.T)
    copies[-1].wait()
    g = go[...]
    packed[C_WO : C_WO + 1, :] = total(g * g + EPS_SQUARE)
    value = packed[...]
    for n in range(send.shape[0]):
        send[n] = value


def wi_places():
    for k in range(W_MATS):
        for b in range(W_COL_TILES):
            lo, hi = b * LANES, min((b + 1) * LANES, W_COLS)
            yield k, C_WI + k * W_COL_TILES + b, lo, hi


def row_places():
    for k in range(A_MATS):
        for t in range(A_TILES):
            yield 0, k, t, k * A_TILES + t
    for k in range(W_MATS):
        for t in range(W_TILES):
            yield 1, k, t, R_WI + k * W_TILES + t


def rows_kernel(ga, gw, go, pa, pw, po, ar, wr, orr, ac, wc, oc, ta, to, packed, old_rows, old_cols, qa, qw, qo, sums, sems):
    copies = grad_copies((pa, pw, po), (qa, qw, qo), sems)
    for c in copies:
        c.start()
    old_rows[...] = jnp.zeros_like(old_rows)
    for which, k, t, at in row_places():
        old_rows[at : at + 1, :] = (ar, wr)[which][k : k + 1, t * LANES : (t + 1) * LANES]
    old_rows[R_WO:R_ALL, :] = orr[...]
    old_cols[...] = jnp.ones_like(old_cols)
    old_cols[0:A_MATS, :] = ac[...]
    for k, at, lo, hi in wi_places():
        old_cols[at : at + 1, 0 : hi - lo] = wc[k : k + 1, lo:hi]
    old_cols[C_WO : C_WO + 1, :] = oc[...]
    for k in range(A_MATS):
        for t in range(A_TILES):
            tile = slice(t * LANES, (t + 1) * LANES)
            g = ga[k, tile, :].T
            ta[k, tile, :] = g
            at = k * A_TILES + t
            packed[at : at + 1, :] = total(g * g + EPS_SQUARE)
    for t in range(O_TILES):
        tile = slice(t * LANES, (t + 1) * LANES)
        g = go[tile, :].T
        to[tile, :] = g
        packed[R_WO + t : R_WO + t + 1, :] = total(g * g + EPS_SQUARE)
    for k in range(W_MATS):
        for t in range(W_TILES):
            g = gw[k, :, t * LANES : (t + 1) * LANES]
            at = R_WI + k * W_TILES + t
            packed[at : at + 1, :] = total(g * g + EPS_SQUARE)
    sums[...] = jnp.zeros_like(sums)
    for k in range(A_MATS):
        copies[k].wait()
        p = qa[k]
        sums[k : k + 1, :] = total(p * p)
    for k in range(W_MATS):
        copies[A_MATS + k].wait()
        folded = jnp.zeros((W_COLS, LANES), jnp.float32)
        for t in range(W_TILES):
            p = qw[k, :, t * LANES : (t + 1) * LANES]
            folded = folded + p * p
        sums[A_MATS + k : A_MATS + k + 1, :] = total(folded)
    copies[-1].wait()
    p = qo[...]
    sums[N_MATS - 1 : N_MATS, :] = total(p * p)
    each = jnp.sum(sums[...], axis=1, keepdims=True)
    sub = lax.broadcasted_iota(jnp.int32, (8, LANES), 0)
    lane = lax.broadcasted_iota(jnp.int32, (8, LANES), 1)
    packed[R_ALL : R_ALL + 1, :] = total(jnp.where(sub == lane, each, 0.0))
    packed[R_ALL + 1 :, :] = jnp.zeros((packed.shape[0] - R_ALL - 1, LANES), jnp.float32)


def cols_kernel(got, old_cols, row_sums, ta, gw, to, send, cols, packed):
    tot = got[0]
    for n in range(1, got.shape[0]):
        tot = tot + got[n]
    at = lax.broadcasted_iota(jnp.int32, (C_ALL, LANES), 0)
    full_a, full_o = float(A_ROWS * got.shape[0]), float(O_ROWS * got.shape[0])
    mean = tot / jnp.where(at == C_WO, full_o, full_a)
    new = BETA * old_cols[...] + (1.0 - BETA) * mean
    cols[...] = new
    inv = 1.0 / new
    packed[0:R_ALL, :] = row_sums[0:R_ALL, :]
    packed[S_PARAM:S_ALL, :] = row_sums[R_ALL : R_ALL + S_ALL - S_PARAM, :]
    for k in range(A_MATS):
        weight = as_column(inv[k : k + 1, :])
        for t in range(A_TILES):
            at = R_ALL + k * A_TILES + t
            g = ta[k, t * LANES : (t + 1) * LANES, :]
            packed[at : at + 1, :] = total(g * g * weight)
    weight = as_column(inv[C_WO : C_WO + 1, :])
    for t in range(O_TILES):
        at = R_ALL + R_WO + t
        g = to[t * LANES : (t + 1) * LANES, :]
        packed[at : at + 1, :] = total(g * g * weight)
    for k in range(W_MATS):
        sums = [jnp.zeros((8, LANES), jnp.float32) for _ in range(W_TILES)]
        for b in range(W_COL_TILES):
            lo, hi = b * LANES, min((b + 1) * LANES, W_COLS)
            at = C_WI + k * W_COL_TILES + b
            weight = as_column(inv[at : at + 1, :])[0 : hi - lo, :]
            for t in range(W_TILES):
                g = gw[k, lo:hi, t * LANES : (t + 1) * LANES]
                part = (g * g * weight).reshape((hi - lo) // 8, 8, LANES)
                sums[t] = sums[t] + jnp.sum(part, axis=0)
        for t in range(W_TILES):
            at = R_ALL + R_WI + k * W_TILES + t
            packed[at : at + 1, :] = total(sums[t])
    send[...] = packed[...]


def sum4_kernel(own, third, second, first, send):
    send[...] = (own[...] + first[...]) + (second[...] + third[...])


def sum4_and_kernel(done, *refs):
    sum4_kernel(*refs)


def new_rows_kernel(n_col, old_rows, own, other, send, rows, tot, ratio):
    tot[...] = own[...] + other[...]
    at = lax.broadcasted_iota(jnp.int32, (R_ALL, LANES), 0)
    full_a, full_w = float(LANES * n_col), float(W_COLS * n_col)
    full = jnp.where((at >= R_WI) & (at < R_WO), full_w, full_a)
    new = BETA * old_rows[0:R_ALL, :] + (1.0 - BETA) * (tot[0:R_ALL, :] / full)
    rows[0:R_ALL, :] = new
    rows[R_ALL:, :] = jnp.ones((rows.shape[0] - R_ALL, LANES), jnp.float32)
    ratio[...] = tot[R_ALL : 2 * R_ALL, :] / new
    spans = [(k * A_TILES, (k + 1) * A_TILES) for k in range(A_MATS)]
    spans += [(R_WI + k * W_TILES, R_WI + (k + 1) * W_TILES) for k in range(W_MATS)]
    spans += [(R_WO, R_ALL)]
    sub = lax.broadcasted_iota(jnp.int32, (8, LANES), 0)
    lane = lax.broadcasted_iota(jnp.int32, (8, LANES), 1)
    levels = jnp.zeros((8, LANES), jnp.float32)
    ratios = jnp.zeros((8, LANES), jnp.float32)
    for k, (lo, hi) in enumerate(spans):
        levels = jnp.where(sub == k, total(rows[lo:hi, :]), levels)
        ratios = jnp.where(sub == k, total(ratio[lo:hi, :]), ratios)
    params = jnp.where(sub == lane, tot[S_PARAM : S_PARAM + 1, :], 0.0)
    levels = jnp.sum(levels, axis=1, keepdims=True)
    ratios = jnp.sum(ratios, axis=1, keepdims=True)
    params = jnp.sum(params, axis=1, keepdims=True)
    value = total(
        jnp.where(lane == sub, levels, 0.0)
        + jnp.where(lane == sub + 32, ratios, 0.0)
        + jnp.where(lane == sub + 64, params, 0.0)
    )
    for n in range(send.shape[0]):
        send[n] = value


def scaled_kernel(ta, gw, to, cols, after, ua, uw, uo, ac, wc, oc, done):
    done[...] = jnp.zeros_like(done)
    ac[...] = cols[0:A_MATS, :]
    for k, at, lo, hi in wi_places():
        wc[k : k + 1, lo:hi] = cols[at : at + 1, 0 : hi - lo]
    oc[...] = cols[C_WO : C_WO + 1, :]
    right = lax.rsqrt(cols[...])
    for k in range(A_MATS):
        column = as_column(right[k : k + 1, :])
        for t in range(A_TILES):
            tile = slice(t * LANES, (t + 1) * LANES)
            ua[k, tile, :] = ta[k, tile, :] * column
    column = as_column(right[C_WO : C_WO + 1, :])
    for t in range(O_TILES):
        tile = slice(t * LANES, (t + 1) * LANES)
        uo[tile, :] = to[tile, :] * column
    for k, at, lo, hi in wi_places():
        column = as_column(right[at : at + 1, :])[0 : hi - lo, :]
        for t in range(W_TILES):
            tile = slice(t * LANES, (t + 1) * LANES)
            uw[k, lo:hi, tile] = gw[k, lo:hi, tile] * column


def update_kernel(n_col, got, rows, ua, uw, uo, a, w, o, ar, wr, orr, va, vw, vo, var, vwr, sems):
    small = [(var, ar), (vwr, wr), (rows.at[R_WO:R_ALL, :], orr)]
    copies = [pltpu.make_async_copy(s, t, sems.at[i]) for i, (s, t) in enumerate(small)]
    for which, k, t, at in row_places():
        (var, vwr)[which][k : k + 1, t * LANES : (t + 1) * LANES] = rows[at : at + 1, :]
    for c in copies:
        c.start()

    def write(source, target):
        copies.append(pltpu.make_async_copy(source, target, sems.at[len(copies)]))
        copies[-1].start()

    left = lax.rsqrt(rows[0:R_ALL, :])
    tot = got[0]
    for n in range(1, got.shape[0]):
        tot = tot + got[n]
    sub = lax.broadcasted_iota(jnp.int32, (8, LANES), 0)
    lane = lax.broadcasted_iota(jnp.int32, (8, LANES), 1)
    levels, ratios, params = (
        jnp.sum(jnp.where(lane == sub + at, tot, 0.0), axis=1, keepdims=True) for at in (0, 32, 64)
    )
    sub = lax.broadcasted_iota(jnp.int32, (8, 1), 0)
    n_row = got.shape[0]
    full_rows = jnp.where(sub == N_MATS - 1, float(O_ROWS * n_row), float(A_ROWS * n_row))
    wide = (sub >= A_MATS) & (sub < A_MATS + W_MATS)
    full_cols = jnp.where(wide, float(W_COLS * n_col), float(LANES * n_col))
    count = full_rows * full_cols
    level = levels / full_rows
    dir_rms = jnp.sqrt(level * ratios / count)
    param_rms = jnp.sqrt(params / count)
    factor = -RHO * param_rms / jnp.maximum(1.0, dir_rms) * jnp.sqrt(level)
    for k in range(W_MATS):
        f = factor[A_MATS + k : A_MATS + k + 1, :]
        scale = [left[R_WI + k * W_TILES + t : R_WI + k * W_TILES + t + 1, :] * f for t in range(W_TILES)]
        for lo, hi in ((0, W_COLS // 2), (W_COLS // 2, W_COLS)):
            for t in range(W_TILES):
                tile = slice(t * LANES, (t + 1) * LANES)
                vw[k, lo:hi, tile] = uw[k, lo:hi, tile] * scale[t]
            write(vw.at[k, lo:hi], w.at[k, lo:hi])
    for k in range(A_MATS):
        f = factor[k : k + 1, :]
        for t in range(A_TILES):
            at = k * A_TILES + t
            tile = slice(t * LANES, (t + 1) * LANES)
            va[k, tile, :] = (ua[k, tile, :] * (left[at : at + 1, :] * f)).T
            if t % 2:
                half = slice((t - 1) * LANES, (t + 1) * LANES)
                write(va.at[k, half], a.at[k, half])
    f = factor[N_MATS - 1 : N_MATS, :]
    for t in range(O_TILES):
        at = R_WO + t
        tile = slice(t * LANES, (t + 1) * LANES)
        vo[tile, :] = (uo[tile, :] * (left[at : at + 1, :] * f)).T
        if t % 2:
            half = slice((t - 1) * LANES, (t + 1) * LANES)
            write(vo.at[half], o.at[half])
    for c in copies:
        c.wait()


def exchange(x, axes):
    return lax.all_to_all(x, axes, 0, 0)


def quad(x, axis, pairings):
    indices = range(lax.axis_size(axis))
    got = [lax.ppermute(x, axis, [(i, i ^ bits) for i in indices]) for bits in pairings]
    return [x] + got[::-1]


def mirror(x, axis):
    n = lax.axis_size(axis)
    return lax.ppermute(x, axis, [(i, n - 1 - i) for i in range(n)])


def shards(
    attn_grad,
    attn_param,
    attn_rows,
    attn_cols,
    wi_grad,
    wi_param,
    wi_rows,
    wi_cols,
    wo_grad,
    wo_param,
    wo_rows,
    wo_cols,
):
    n_row, n_col = lax.axis_size(ROW), lax.axis_size(COL)
    wi_grad = jnp.swapaxes(wi_grad, 1, 2)
    wi_param = jnp.swapaxes(wi_param, 1, 2)
    blocks = ((A_MATS, A_ROWS, LANES), (W_MATS, W_COLS, W_ROWS), (O_ROWS, LANES))
    held = [vmem(*b) for b in blocks]
    sems = pltpu.SemaphoreType.DMA((N_MATS,))
    send, ga, gw, go = call(
        load_kernel,
        [f32(n_row, C_ALL, LANES)] + held,
        [ANYWHERE] * 3,
        [WHOLE] * 4,
        [vmem(C_ALL, LANES), sems],
        bytes_accessed=3 << 20,
    )(far(attn_grad), far(wi_grad), far(wo_grad))
    got = exchange(send, ROW)
    ga, gw, go = here(ga), here(gw), here(go)
    ta, to, row_sums, old_rows, old_cols = call(
        rows_kernel,
        [held[0], held[2], vmem(40, LANES), vmem(40, LANES), vmem(C_ALL, LANES)],
        [WHOLE] * 3 + [ANYWHERE] * 3 + [WHOLE] * 6,
        [WHOLE] * 5,
        held + [vmem(8, LANES), sems],
        bytes_accessed=6 << 20,
        aliases={0: 0, 2: 1},
    )(
        ga,
        gw,
        go,
        far(attn_param),
        far(wi_param),
        far(wo_param),
        attn_rows,
        wi_rows,
        wo_rows.reshape(O_TILES, LANES),
        attn_cols,
        wi_cols,
        wo_cols.reshape(1, LANES),
    )
    ta, to = here(ta), here(to)
    send, cols = call(
        cols_kernel,
        [f32(S_ALL, LANES), vmem(C_ALL, LANES)],
        [WHOLE] * 6,
        [WHOLE] * 2,
        [vmem(S_ALL, LANES)],
        bytes_accessed=3 << 20,
    )(got, here(old_cols), here(row_sums), ta, gw, to)
    got = quad(send, "z", (3, 2, 1))
    send = call(sum4_kernel, f32(S_ALL, LANES), [WHOLE] * 4, WHOLE)(*got)
    got = quad(send, "x", (2, 3, 1))
    ua, uw, uo, attn_cols_new, wi_cols_new, wo_cols_new, done = call(
        scaled_kernel,
        held + [f32(A_MATS, LANES), f32(W_MATS, W_COLS), f32(1, LANES), vmem(8, LANES)],
        [WHOLE] * 4 + [ANYWHERE],
        [WHOLE] * 7,
        bytes_accessed=6 << 20,
        aliases={0: 0, 1: 1, 2: 2},
    )(ta, gw, to, here(cols), send)
    send = call(sum4_and_kernel, f32(S_ALL, LANES), [ANYWHERE] + [WHOLE] * 4, WHOLE)(here(done), *got)
    got = mirror(send, "z")
    send, rows = call(
        lambda *refs: new_rows_kernel(n_col, *refs),
        [f32(n_row, 1, LANES), vmem(40, LANES)],
        [WHOLE] * 3,
        [WHOLE] * 2,
        [vmem(S_ALL, LANES), vmem(R_ALL, LANES)],
    )(here(old_rows), send, got)
    got = exchange(send, ROW)
    attn_update, wi_update, wo_update, attn_rows_new, wi_rows_new, wo_rows_new = call(
        lambda *refs: update_kernel(n_col, *refs),
        [hbm(*b) for b in blocks] + [hbm(A_MATS, A_ROWS), hbm(W_MATS, W_ROWS), hbm(O_TILES, LANES)],
        [WHOLE] * 5,
        [ANYWHERE] * 6,
        held + [vmem(A_MATS, A_ROWS), vmem(W_MATS, W_ROWS), pltpu.SemaphoreType.DMA((N_WRITES,))],
        bytes_accessed=3 << 20,
    )(got, here(rows), here(ua), here(uw), here(uo))
    return (
        attn_update,
        attn_rows_new,
        attn_cols_new,
        jnp.swapaxes(wi_update, 1, 2),
        wi_rows_new,
        wi_cols_new,
        wo_update,
        wo_rows_new.reshape(O_ROWS),
        wo_cols_new.reshape(LANES),
    )


def solution(mesh):
    fine = Mesh(mesh.devices.reshape(4, 2, 4, 8), ROW + COL)
    big, row, col = P(None, ROW, COL), P(None, ROW), P(None, COL)
    return jax.shard_map(
        shards,
        mesh=fine,
        in_specs=(big, big, row, col, big, big, row, col, P(ROW, COL), P(ROW, COL), P(ROW), P(COL)),
        out_specs=(big, row, col, big, row, col, P(ROW, COL), P(ROW), P(COL)),
        check_vma=False,
    )
```

```python
import jax
import jax.numpy as jnp
from jax import lax
from jax.experimental import pallas as pl
from jax.experimental.pallas import tpu as pltpu
from jax.sharding import Mesh, PartitionSpec as P

STEP = 2
EPS_SQUARE = 1e-30
BETA = 1.0 - STEP ** (-0.8)
RHO = STEP ** (-0.5)
LANES = 128
N_MATS = 7

ROW = ("y", "core")
COL = ("x", "z")

A_MATS, A_ROWS = 4, 512
W_MATS, W_COLS, W_ROWS = 2, 320, 512
O_ROWS = 1280
A_TILES, O_TILES, W_TILES = A_ROWS // LANES, O_ROWS // LANES, W_ROWS // LANES
W_COL_TILES = -(-W_COLS // LANES)

C_WI, C_WO, C_SENT, C_ALL = 4, 10, 11, 16
R_WI, R_WO, R_ALL = 16, 24, 34
S_PARAM, S_ALL = 2 * R_ALL, 72

N_WRITES = 3 + 2 * W_MATS + (A_MATS * A_TILES + O_TILES) // 2

VMEM_LIMIT = 48 * 1024 * 1024
WHOLE = pl.BlockSpec(memory_space=pltpu.VMEM)
ANYWHERE = pl.BlockSpec(memory_space=pl.ANY)


def call(body, out_shape, in_specs, out_specs, scratch=(), bytes_accessed=1 << 20, aliases=None):
    return pl.pallas_call(
        body,
        out_shape=out_shape,
        in_specs=in_specs,
        out_specs=out_specs,
        scratch_shapes=list(scratch),
        input_output_aliases=aliases or {},
        compiler_params=pltpu.CompilerParams(vmem_limit_bytes=VMEM_LIMIT),
        cost_estimate=pl.CostEstimate(flops=4 << 20, bytes_accessed=bytes_accessed, transcendentals=0),
    )


def here(x):
    return pltpu.with_memory_space_constraint(x, pltpu.VMEM)


def far(x):
    return pltpu.with_memory_space_constraint(x, pltpu.HBM)


def f32(*shape):
    return jax.ShapeDtypeStruct(shape, jnp.float32)


def vmem(*shape):
    return pltpu.VMEM(shape, jnp.float32)


def hbm(*shape):
    return pltpu.HBM(shape, jnp.float32)


def grad_copies(sources, targets, sems):
    a, w, o = sources
    a_to, w_to, o_to = targets
    pairs = [(a.at[k], a_to.at[k]) for k in range(A_MATS)]
    pairs += [(w.at[k], w_to.at[k]) for k in range(W_MATS)]
    pairs += [(o, o_to)]
    return [pltpu.make_async_copy(s, t, sems.at[i]) for i, (s, t) in enumerate(pairs)]


def total(x):
    return jnp.sum(x, axis=0, keepdims=True)


def as_column(row):
    return jnp.broadcast_to(row, (LANES, LANES)).T


def load_kernel(a, w, o, send, ga, gw, go, packed, sems):
    copies = grad_copies((a, w, o), (ga, gw, go), sems)
    for c in copies:
        c.start()
    packed[...] = jnp.zeros_like(packed)
    for k in range(A_MATS):
        copies[k].wait()
        g = ga[k]
        packed[k : k + 1, :] = total(g * g + EPS_SQUARE)
    for k in range(W_MATS):
        copies[A_MATS + k].wait()
        for b in range(W_COL_TILES):
            lo, hi = b * LANES, min((b + 1) * LANES, W_COLS)
            folded = jnp.zeros((hi - lo, LANES), jnp.float32)
            for t in range(W_TILES):
                g = gw[k, lo:hi, t * LANES : (t + 1) * LANES]
                folded = folded + (g * g + EPS_SQUARE)
            if hi - lo < LANES:
                folded = jnp.concatenate([folded, jnp.zeros((LANES - hi + lo, LANES), jnp.float32)], axis=0)
            at = C_WI + k * W_COL_TILES + b
            packed[at : at + 1, :] = total(folded.T)
    copies[-1].wait()
    g = go[...]
    packed[C_WO : C_WO + 1, :] = total(g * g + EPS_SQUARE)
    for i in range(C_SENT):
        row = packed[i : i + 1, :]
        for n in range(send.shape[0]):
            send[n, :, i * LANES : (i + 1) * LANES] = row


def wi_places():
    for k in range(W_MATS):
        for b in range(W_COL_TILES):
            lo, hi = b * LANES, min((b + 1) * LANES, W_COLS)
            yield k, C_WI + k * W_COL_TILES + b, lo, hi


def row_places():
    for k in range(A_MATS):
        for t in range(A_TILES):
            yield 0, k, t, k * A_TILES + t
    for k in range(W_MATS):
        for t in range(W_TILES):
            yield 1, k, t, R_WI + k * W_TILES + t


def rows_kernel(ga, gw, go, pa, pw, po, ar, wr, orr, ac, wc, oc, ta, to, packed, old_rows, old_cols, qa, qw, qo, sums, sems):
    copies = grad_copies((pa, pw, po), (qa, qw, qo), sems)
    for c in copies:
        c.start()
    old_rows[...] = jnp.zeros_like(old_rows)
    for which, k, t, at in row_places():
        old_rows[at : at + 1, :] = (ar, wr)[which][k : k + 1, t * LANES : (t + 1) * LANES]
    old_rows[R_WO:R_ALL, :] = orr[...]
    old_cols[...] = jnp.ones_like(old_cols)
    old_cols[0:A_MATS, :] = ac[...]
    for k, at, lo, hi in wi_places():
        old_cols[at : at + 1, 0 : hi - lo] = wc[k : k + 1, lo:hi]
    old_cols[C_WO : C_WO + 1, :] = oc[...]
    for k in range(A_MATS):
        for t in range(A_TILES):
            tile = slice(t * LANES, (t + 1) * LANES)
            g = ga[k, tile, :].T
            ta[k, tile, :] = g
            at = k * A_TILES + t
            packed[at : at + 1, :] = total(g * g + EPS_SQUARE)
    for t in range(O_TILES):
        tile = slice(t * LANES, (t + 1) * LANES)
        g = go[tile, :].T
        to[tile, :] = g
        packed[R_WO + t : R_WO + t + 1, :] = total(g * g + EPS_SQUARE)
    for k in range(W_MATS):
        for t in range(W_TILES):
            g = gw[k, :, t * LANES : (t + 1) * LANES]
            at = R_WI + k * W_TILES + t
            packed[at : at + 1, :] = total(g * g + EPS_SQUARE)
    sums[...] = jnp.zeros_like(sums)
    for k in range(A_MATS):
        copies[k].wait()
        p = qa[k]
        sums[k : k + 1, :] = total(p * p)
    for k in range(W_MATS):
        copies[A_MATS + k].wait()
        folded = jnp.zeros((W_COLS, LANES), jnp.float32)
        for t in range(W_TILES):
            p = qw[k, :, t * LANES : (t + 1) * LANES]
            folded = folded + p * p
        sums[A_MATS + k : A_MATS + k + 1, :] = total(folded)
    copies[-1].wait()
    p = qo[...]
    sums[N_MATS - 1 : N_MATS, :] = total(p * p)
    each = jnp.sum(sums[...], axis=1, keepdims=True)
    sub = lax.broadcasted_iota(jnp.int32, (8, LANES), 0)
    lane = lax.broadcasted_iota(jnp.int32, (8, LANES), 1)
    packed[R_ALL : R_ALL + 1, :] = total(jnp.where(sub == lane, each, 0.0))
    packed[R_ALL + 1 :, :] = jnp.zeros((packed.shape[0] - R_ALL - 1, LANES), jnp.float32)


def cols_kernel(got, old_cols, row_sums, ta, gw, to, send, cols, packed):
    flat = got[0]
    for n in range(1, got.shape[0]):
        flat = flat + got[n]
    cols[...] = jnp.zeros_like(cols)
    for i in range(C_SENT):
        cols[i : i + 1, :] = flat[:, i * LANES : (i + 1) * LANES]
    tot = cols[...]
    at = lax.broadcasted_iota(jnp.int32, (C_ALL, LANES), 0)
    full_a, full_o = float(A_ROWS * got.shape[0]), float(O_ROWS * got.shape[0])
    mean = tot / jnp.where(at == C_WO, full_o, full_a)
    new = BETA * old_cols[...] + (1.0 - BETA) * mean
    cols[...] = new
    inv = 1.0 / new
    packed[0:R_ALL, :] = row_sums[0:R_ALL, :]
    packed[S_PARAM:S_ALL, :] = row_sums[R_ALL : R_ALL + S_ALL - S_PARAM, :]
    for k in range(A_MATS):
        weight = as_column(inv[k : k + 1, :])
        for t in range(A_TILES):
            at = R_ALL + k * A_TILES + t
            g = ta[k, t * LANES : (t + 1) * LANES, :]
            packed[at : at + 1, :] = total(g * g * weight)
    weight = as_column(inv[C_WO : C_WO + 1, :])
    for t in range(O_TILES):
        at = R_ALL + R_WO + t
        g = to[t * LANES : (t + 1) * LANES, :]
        packed[at : at + 1, :] = total(g * g * weight)
    for k in range(W_MATS):
        sums = [jnp.zeros((8, LANES), jnp.float32) for _ in range(W_TILES)]
        for b in range(W_COL_TILES):
            lo, hi = b * LANES, min((b + 1) * LANES, W_COLS)
            at = C_WI + k * W_COL_TILES + b
            weight = as_column(inv[at : at + 1, :])[0 : hi - lo, :]
            for t in range(W_TILES):
                g = gw[k, lo:hi, t * LANES : (t + 1) * LANES]
                part = (g * g * weight).reshape((hi - lo) // 8, 8, LANES)
                sums[t] = sums[t] + jnp.sum(part, axis=0)
        for t in range(W_TILES):
            at = R_ALL + R_WI + k * W_TILES + t
            packed[at : at + 1, :] = total(sums[t])
    send[...] = packed[...]


def sum4_kernel(own, third, second, first, send):
    send[...] = (own[...] + first[...]) + (second[...] + third[...])


def sum4_and_kernel(done, *refs):
    sum4_kernel(*refs)


def new_rows_kernel(n_col, old_rows, own, other, send, rows, tot, ratio):
    tot[...] = own[...] + other[...]
    at = lax.broadcasted_iota(jnp.int32, (R_ALL, LANES), 0)
    full_a, full_w = float(LANES * n_col), float(W_COLS * n_col)
    full = jnp.where((at >= R_WI) & (at < R_WO), full_w, full_a)
    new = BETA * old_rows[0:R_ALL, :] + (1.0 - BETA) * (tot[0:R_ALL, :] / full)
    rows[0:R_ALL, :] = new
    rows[R_ALL:, :] = jnp.ones((rows.shape[0] - R_ALL, LANES), jnp.float32)
    ratio[...] = tot[R_ALL : 2 * R_ALL, :] / new
    spans = [(k * A_TILES, (k + 1) * A_TILES) for k in range(A_MATS)]
    spans += [(R_WI + k * W_TILES, R_WI + (k + 1) * W_TILES) for k in range(W_MATS)]
    spans += [(R_WO, R_ALL)]
    sub = lax.broadcasted_iota(jnp.int32, (8, LANES), 0)
    lane = lax.broadcasted_iota(jnp.int32, (8, LANES), 1)
    levels = jnp.zeros((8, LANES), jnp.float32)
    ratios = jnp.zeros((8, LANES), jnp.float32)
    for k, (lo, hi) in enumerate(spans):
        levels = jnp.where(sub == k, total(rows[lo:hi, :]), levels)
        ratios = jnp.where(sub == k, total(ratio[lo:hi, :]), ratios)
    params = jnp.where(sub == lane, tot[S_PARAM : S_PARAM + 1, :], 0.0)
    levels = jnp.sum(levels, axis=1, keepdims=True)
    ratios = jnp.sum(ratios, axis=1, keepdims=True)
    params = jnp.sum(params, axis=1, keepdims=True)
    value = total(
        jnp.where(lane == sub, levels, 0.0)
        + jnp.where(lane == sub + 32, ratios, 0.0)
        + jnp.where(lane == sub + 64, params, 0.0)
    )
    for n in range(send.shape[0]):
        send[n] = value


def scaled_kernel(ta, gw, to, cols, after, ua, uw, uo, ac, wc, oc, done):
    done[...] = jnp.zeros_like(done)
    ac[...] = cols[0:A_MATS, :]
    for k, at, lo, hi in wi_places():
        wc[k : k + 1, lo:hi] = cols[at : at + 1, 0 : hi - lo]
    oc[...] = cols[C_WO : C_WO + 1, :]
    right = lax.rsqrt(cols[...])
    for k in range(A_MATS):
        column = as_column(right[k : k + 1, :])
        for t in range(A_TILES):
            tile = slice(t * LANES, (t + 1) * LANES)
            ua[k, tile, :] = ta[k, tile, :] * column
    column = as_column(right[C_WO : C_WO + 1, :])
    for t in range(O_TILES):
        tile = slice(t * LANES, (t + 1) * LANES)
        uo[tile, :] = to[tile, :] * column
    for k, at, lo, hi in wi_places():
        column = as_column(right[at : at + 1, :])[0 : hi - lo, :]
        for t in range(W_TILES):
            tile = slice(t * LANES, (t + 1) * LANES)
            uw[k, lo:hi, tile] = gw[k, lo:hi, tile] * column


def update_kernel(n_col, got, rows, ua, uw, uo, a, w, o, ar, wr, orr, va, vw, vo, var, vwr, sems):
    small = [(var, ar), (vwr, wr), (rows.at[R_WO:R_ALL, :], orr)]
    copies = [pltpu.make_async_copy(s, t, sems.at[i]) for i, (s, t) in enumerate(small)]
    for which, k, t, at in row_places():
        (var, vwr)[which][k : k + 1, t * LANES : (t + 1) * LANES] = rows[at : at + 1, :]
    for c in copies:
        c.start()

    def write(source, target):
        copies.append(pltpu.make_async_copy(source, target, sems.at[len(copies)]))
        copies[-1].start()

    left = lax.rsqrt(rows[0:R_ALL, :])
    tot = got[0]
    for n in range(1, got.shape[0]):
        tot = tot + got[n]
    sub = lax.broadcasted_iota(jnp.int32, (8, LANES), 0)
    lane = lax.broadcasted_iota(jnp.int32, (8, LANES), 1)
    levels, ratios, params = (
        jnp.sum(jnp.where(lane == sub + at, tot, 0.0), axis=1, keepdims=True) for at in (0, 32, 64)
    )
    sub = lax.broadcasted_iota(jnp.int32, (8, 1), 0)
    n_row = got.shape[0]
    full_rows = jnp.where(sub == N_MATS - 1, float(O_ROWS * n_row), float(A_ROWS * n_row))
    wide = (sub >= A_MATS) & (sub < A_MATS + W_MATS)
    full_cols = jnp.where(wide, float(W_COLS * n_col), float(LANES * n_col))
    count = full_rows * full_cols
    level = levels / full_rows
    dir_rms = jnp.sqrt(level * ratios / count)
    param_rms = jnp.sqrt(params / count)
    factor = -RHO * param_rms / jnp.maximum(1.0, dir_rms) * jnp.sqrt(level)
    for k in range(W_MATS):
        f = factor[A_MATS + k : A_MATS + k + 1, :]
        scale = [left[R_WI + k * W_TILES + t : R_WI + k * W_TILES + t + 1, :] * f for t in range(W_TILES)]
        for lo, hi in ((0, W_COLS // 2), (W_COLS // 2, W_COLS)):
            for t in range(W_TILES):
                tile = slice(t * LANES, (t + 1) * LANES)
                vw[k, lo:hi, tile] = uw[k, lo:hi, tile] * scale[t]
            write(vw.at[k, lo:hi], w.at[k, lo:hi])
    for k in range(A_MATS):
        f = factor[k : k + 1, :]
        for t in range(A_TILES):
            at = k * A_TILES + t
            tile = slice(t * LANES, (t + 1) * LANES)
            va[k, tile, :] = (ua[k, tile, :] * (left[at : at + 1, :] * f)).T
            if t % 2:
                half = slice((t - 1) * LANES, (t + 1) * LANES)
                write(va.at[k, half], a.at[k, half])
    f = factor[N_MATS - 1 : N_MATS, :]
    for t in range(O_TILES):
        at = R_WO + t
        tile = slice(t * LANES, (t + 1) * LANES)
        vo[tile, :] = (uo[tile, :] * (left[at : at + 1, :] * f)).T
        if t % 2:
            half = slice((t - 1) * LANES, (t + 1) * LANES)
            write(vo.at[half], o.at[half])
    for c in copies:
        c.wait()


def exchange(x, axes):
    return lax.all_to_all(x, axes, 0, 0)


def quad(x, axis, pairings):
    indices = range(lax.axis_size(axis))
    got = [lax.ppermute(x, axis, [(i, i ^ bits) for i in indices]) for bits in pairings]
    return [x] + got[::-1]


def mirror(x, axis):
    n = lax.axis_size(axis)
    return lax.ppermute(x, axis, [(i, n - 1 - i) for i in range(n)])


def shards(
    attn_grad,
    attn_param,
    attn_rows,
    attn_cols,
    wi_grad,
    wi_param,
    wi_rows,
    wi_cols,
    wo_grad,
    wo_param,
    wo_rows,
    wo_cols,
):
    n_row, n_col = lax.axis_size(ROW), lax.axis_size(COL)
    wi_grad = jnp.swapaxes(wi_grad, 1, 2)
    wi_param = jnp.swapaxes(wi_param, 1, 2)
    blocks = ((A_MATS, A_ROWS, LANES), (W_MATS, W_COLS, W_ROWS), (O_ROWS, LANES))
    held = [vmem(*b) for b in blocks]
    sems = pltpu.SemaphoreType.DMA((N_MATS,))
    send, ga, gw, go = call(
        load_kernel,
        [f32(n_row, 1, C_SENT * LANES)] + held,
        [ANYWHERE] * 3,
        [WHOLE] * 4,
        [vmem(C_ALL, LANES), sems],
        bytes_accessed=3 << 20,
    )(far(attn_grad), far(wi_grad), far(wo_grad))
    got = exchange(send, ROW)
    ga, gw, go = here(ga), here(gw), here(go)
    ta, to, row_sums, old_rows, old_cols = call(
        rows_kernel,
        [held[0], held[2], vmem(40, LANES), vmem(40, LANES), vmem(C_ALL, LANES)],
        [WHOLE] * 3 + [ANYWHERE] * 3 + [WHOLE] * 6,
        [WHOLE] * 5,
        held + [vmem(8, LANES), sems],
        bytes_accessed=6 << 20,
        aliases={0: 0, 2: 1},
    )(
        ga,
        gw,
        go,
        far(attn_param),
        far(wi_param),
        far(wo_param),
        attn_rows,
        wi_rows,
        wo_rows.reshape(O_TILES, LANES),
        attn_cols,
        wi_cols,
        wo_cols.reshape(1, LANES),
    )
    ta, to = here(ta), here(to)
    send, cols = call(
        cols_kernel,
        [f32(S_ALL, LANES), vmem(C_ALL, LANES)],
        [WHOLE] * 6,
        [WHOLE] * 2,
        [vmem(S_ALL, LANES)],
        bytes_accessed=3 << 20,
    )(got, here(old_cols), here(row_sums), ta, gw, to)
    got = quad(send, "z", (3, 2, 1))
    send = call(sum4_kernel, f32(S_ALL, LANES), [WHOLE] * 4, WHOLE)(*got)
    got = quad(send, "x", (2, 3, 1))
    ua, uw, uo, attn_cols_new, wi_cols_new, wo_cols_new, done = call(
        scaled_kernel,
        held + [f32(A_MATS, LANES), f32(W_MATS, W_COLS), f32(1, LANES), vmem(8, LANES)],
        [WHOLE] * 4 + [ANYWHERE],
        [WHOLE] * 7,
        bytes_accessed=6 << 20,
        aliases={0: 0, 1: 1, 2: 2},
    )(ta, gw, to, here(cols), send)
    send = call(sum4_and_kernel, f32(S_ALL, LANES), [ANYWHERE] + [WHOLE] * 4, WHOLE)(here(done), *got)
    got = mirror(send, "z")
    send, rows = call(
        lambda *refs: new_rows_kernel(n_col, *refs),
        [f32(n_row, 1, LANES), vmem(40, LANES)],
        [WHOLE] * 3,
        [WHOLE] * 2,
        [vmem(S_ALL, LANES), vmem(R_ALL, LANES)],
    )(here(old_rows), send, got)
    got = exchange(send, ROW)
    attn_update, wi_update, wo_update, attn_rows_new, wi_rows_new, wo_rows_new = call(
        lambda *refs: update_kernel(n_col, *refs),
        [hbm(*b) for b in blocks] + [hbm(A_MATS, A_ROWS), hbm(W_MATS, W_ROWS), hbm(O_TILES, LANES)],
        [WHOLE] * 5,
        [ANYWHERE] * 6,
        held + [vmem(A_MATS, A_ROWS), vmem(W_MATS, W_ROWS), pltpu.SemaphoreType.DMA((N_WRITES,))],
        bytes_accessed=3 << 20,
    )(got, here(rows), here(ua), here(uw), here(uo))
    return (
        attn_update,
        attn_rows_new,
        attn_cols_new,
        jnp.swapaxes(wi_update, 1, 2),
        wi_rows_new,
        wi_cols_new,
        wo_update,
        wo_rows_new.reshape(O_ROWS),
        wo_cols_new.reshape(LANES),
    )


def solution(mesh):
    fine = Mesh(mesh.devices.reshape(4, 2, 4, 8), ROW + COL)
    big, row, col = P(None, ROW, COL), P(None, ROW), P(None, COL)
    return jax.shard_map(
        shards,
        mesh=fine,
        in_specs=(big, big, row, col, big, big, row, col, P(ROW, COL), P(ROW, COL), P(ROW), P(COL)),
        out_specs=(big, row, col, big, row, col, P(ROW, COL), P(ROW), P(COL)),
        check_vma=False,
    )
```

```python
import jax
import jax.numpy as jnp
from jax import lax
from jax.experimental import pallas as pl
from jax.experimental.pallas import tpu as pltpu
from jax.sharding import Mesh, PartitionSpec as P

STEP = 2
EPS_SQUARE = 1e-30
BETA = 1.0 - STEP ** (-0.8)
RHO = STEP ** (-0.5)
LANES = 128
N_MATS = 7

ROW = ("y", "core")
COL = ("x", "z")

A_MATS, A_ROWS = 4, 512
W_MATS, W_COLS, W_ROWS = 2, 320, 512
O_ROWS = 1280
A_TILES, O_TILES, W_TILES = A_ROWS // LANES, O_ROWS // LANES, W_ROWS // LANES
W_COL_TILES = -(-W_COLS // LANES)

C_WI, C_WO, C_SENT, C_ALL = 4, 10, 11, 16
R_WI, R_WO, R_ALL = 16, 24, 34
S_PARAM, S_ALL = 2 * R_ALL, 72

N_WRITES = 3 + 2 * W_MATS + (A_MATS * A_TILES + O_TILES) // 2

VMEM_LIMIT = 48 * 1024 * 1024
WHOLE = pl.BlockSpec(memory_space=pltpu.VMEM)
ANYWHERE = pl.BlockSpec(memory_space=pl.ANY)


def call(body, out_shape, in_specs, out_specs, scratch=(), bytes_accessed=1 << 20, aliases=None):
    return pl.pallas_call(
        body,
        out_shape=out_shape,
        in_specs=in_specs,
        out_specs=out_specs,
        scratch_shapes=list(scratch),
        input_output_aliases=aliases or {},
        compiler_params=pltpu.CompilerParams(vmem_limit_bytes=VMEM_LIMIT),
        cost_estimate=pl.CostEstimate(flops=4 << 20, bytes_accessed=bytes_accessed, transcendentals=0),
    )


def here(x):
    return pltpu.with_memory_space_constraint(x, pltpu.VMEM)


def far(x):
    return pltpu.with_memory_space_constraint(x, pltpu.HBM)


def f32(*shape):
    return jax.ShapeDtypeStruct(shape, jnp.float32)


def vmem(*shape):
    return pltpu.VMEM(shape, jnp.float32)


def hbm(*shape):
    return pltpu.HBM(shape, jnp.float32)


def grad_copies(sources, targets, sems):
    a, w, o = sources
    a_to, w_to, o_to = targets
    pairs = [(a.at[k], a_to.at[k]) for k in range(A_MATS)]
    pairs += [(w.at[k], w_to.at[k]) for k in range(W_MATS)]
    pairs += [(o, o_to)]
    return [pltpu.make_async_copy(s, t, sems.at[i]) for i, (s, t) in enumerate(pairs)]


def total(x):
    return jnp.sum(x, axis=0, keepdims=True)


def as_column(row):
    return jnp.broadcast_to(row, (LANES, LANES)).T


def load_kernel(a, w, o, send, ga, gw, go, packed, sems):
    copies = grad_copies((a, w, o), (ga, gw, go), sems)
    for c in copies:
        c.start()
    packed[...] = jnp.zeros_like(packed)
    for k in range(A_MATS):
        copies[k].wait()
        g = ga[k]
        packed[k : k + 1, :] = total(g * g + EPS_SQUARE)
    for k in range(W_MATS):
        copies[A_MATS + k].wait()
        for b in range(W_COL_TILES):
            lo, hi = b * LANES, min((b + 1) * LANES, W_COLS)
            folded = jnp.zeros((hi - lo, LANES), jnp.float32)
            for t in range(W_TILES):
                g = gw[k, lo:hi, t * LANES : (t + 1) * LANES]
                folded = folded + (g * g + EPS_SQUARE)
            if hi - lo < LANES:
                folded = jnp.concatenate([folded, jnp.zeros((LANES - hi + lo, LANES), jnp.float32)], axis=0)
            at = C_WI + k * W_COL_TILES + b
            packed[at : at + 1, :] = total(folded.T)
    copies[-1].wait()
    g = go[...]
    packed[C_WO : C_WO + 1, :] = total(g * g + EPS_SQUARE)
    for i in range(C_SENT):
        row = packed[i : i + 1, :]
        for n in range(send.shape[0]):
            send[n, :, i * LANES : (i + 1) * LANES] = row


def wi_places():
    for k in range(W_MATS):
        for b in range(W_COL_TILES):
            lo, hi = b * LANES, min((b + 1) * LANES, W_COLS)
            yield k, C_WI + k * W_COL_TILES + b, lo, hi


def row_places():
    for k in range(A_MATS):
        for t in range(A_TILES):
            yield 0, k, t, k * A_TILES + t
    for k in range(W_MATS):
        for t in range(W_TILES):
            yield 1, k, t, R_WI + k * W_TILES + t


def rows_kernel(ga, gw, go, pa, pw, po, ar, wr, orr, ac, wc, oc, ta, to, packed, old_rows, old_cols, qa, qw, qo, sums, sems):
    copies = grad_copies((pa, pw, po), (qa, qw, qo), sems)
    for c in copies:
        c.start()
    old_rows[...] = jnp.zeros_like(old_rows)
    for which, k, t, at in row_places():
        old_rows[at : at + 1, :] = (ar, wr)[which][k : k + 1, t * LANES : (t + 1) * LANES]
    old_rows[R_WO:R_ALL, :] = orr[...]
    old_cols[...] = jnp.ones_like(old_cols)
    old_cols[0:A_MATS, :] = ac[...]
    for k, at, lo, hi in wi_places():
        old_cols[at : at + 1, 0 : hi - lo] = wc[k : k + 1, lo:hi]
    old_cols[C_WO : C_WO + 1, :] = oc[...]
    for k in range(A_MATS):
        for t in range(A_TILES):
            tile = slice(t * LANES, (t + 1) * LANES)
            g = ga[k, tile, :].T
            ta[k, tile, :] = g
            at = k * A_TILES + t
            packed[at : at + 1, :] = total(g * g + EPS_SQUARE)
    for t in range(O_TILES):
        tile = slice(t * LANES, (t + 1) * LANES)
        g = go[tile, :].T
        to[tile, :] = g
        packed[R_WO + t : R_WO + t + 1, :] = total(g * g + EPS_SQUARE)
    for k in range(W_MATS):
        for t in range(W_TILES):
            g = gw[k, :, t * LANES : (t + 1) * LANES]
            at = R_WI + k * W_TILES + t
            packed[at : at + 1, :] = total(g * g + EPS_SQUARE)
    sums[...] = jnp.zeros_like(sums)
    for k in range(A_MATS):
        copies[k].wait()
        p = qa[k]
        sums[k : k + 1, :] = total(p * p)
    for k in range(W_MATS):
        copies[A_MATS + k].wait()
        folded = jnp.zeros((W_COLS, LANES), jnp.float32)
        for t in range(W_TILES):
            p = qw[k, :, t * LANES : (t + 1) * LANES]
            folded = folded + p * p
        sums[A_MATS + k : A_MATS + k + 1, :] = total(folded)
    copies[-1].wait()
    p = qo[...]
    sums[N_MATS - 1 : N_MATS, :] = total(p * p)
    each = jnp.sum(sums[...], axis=1, keepdims=True)
    sub = lax.broadcasted_iota(jnp.int32, (8, LANES), 0)
    lane = lax.broadcasted_iota(jnp.int32, (8, LANES), 1)
    packed[R_ALL : R_ALL + 1, :] = total(jnp.where(sub == lane, each, 0.0))
    packed[R_ALL + 1 :, :] = jnp.zeros((packed.shape[0] - R_ALL - 1, LANES), jnp.float32)


def cols_kernel(got, old_cols, row_sums, ta, gw, to, send, cols, packed):
    flat = got[0]
    for n in range(1, got.shape[0]):
        flat = flat + got[n]
    cols[...] = jnp.zeros_like(cols)
    for i in range(C_SENT):
        cols[i : i + 1, :] = flat[:, i * LANES : (i + 1) * LANES]
    tot = cols[...]
    at = lax.broadcasted_iota(jnp.int32, (C_ALL, LANES), 0)
    full_a, full_o = float(A_ROWS * got.shape[0]), float(O_ROWS * got.shape[0])
    mean = tot / jnp.where(at == C_WO, full_o, full_a)
    new = BETA * old_cols[...] + (1.0 - BETA) * mean
    cols[...] = new
    inv = 1.0 / new
    packed[0:R_ALL, :] = row_sums[0:R_ALL, :]
    packed[S_PARAM:S_ALL, :] = row_sums[R_ALL : R_ALL + S_ALL - S_PARAM, :]
    for k in range(A_MATS):
        weight = as_column(inv[k : k + 1, :])
        for t in range(A_TILES):
            at = R_ALL + k * A_TILES + t
            g = ta[k, t * LANES : (t + 1) * LANES, :]
            packed[at : at + 1, :] = total(g * g * weight)
    weight = as_column(inv[C_WO : C_WO + 1, :])
    for t in range(O_TILES):
        at = R_ALL + R_WO + t
        g = to[t * LANES : (t + 1) * LANES, :]
        packed[at : at + 1, :] = total(g * g * weight)
    for k in range(W_MATS):
        sums = [jnp.zeros((8, LANES), jnp.float32) for _ in range(W_TILES)]
        for b in range(W_COL_TILES):
            lo, hi = b * LANES, min((b + 1) * LANES, W_COLS)
            at = C_WI + k * W_COL_TILES + b
            weight = as_column(inv[at : at + 1, :])[0 : hi - lo, :]
            for t in range(W_TILES):
                g = gw[k, lo:hi, t * LANES : (t + 1) * LANES]
                part = (g * g * weight).reshape((hi - lo) // 8, 8, LANES)
                sums[t] = sums[t] + jnp.sum(part, axis=0)
        for t in range(W_TILES):
            at = R_ALL + R_WI + k * W_TILES + t
            packed[at : at + 1, :] = total(sums[t])
    send[...] = packed[...]


def sum4_kernel(own, third, second, first, send):
    send[...] = (own[...] + first[...]) + (second[...] + third[...])


def sum4_and_kernel(done, *refs):
    sum4_kernel(*refs)


def new_rows_kernel(n_col, old_rows, own, other, send, rows, tot, ratio):
    tot[...] = own[...] + other[...]
    at = lax.broadcasted_iota(jnp.int32, (R_ALL, LANES), 0)
    full_a, full_w = float(LANES * n_col), float(W_COLS * n_col)
    full = jnp.where((at >= R_WI) & (at < R_WO), full_w, full_a)
    new = BETA * old_rows[0:R_ALL, :] + (1.0 - BETA) * (tot[0:R_ALL, :] / full)
    rows[0:R_ALL, :] = new
    rows[R_ALL:, :] = jnp.ones((rows.shape[0] - R_ALL, LANES), jnp.float32)
    ratio[...] = tot[R_ALL : 2 * R_ALL, :] / new
    spans = [(k * A_TILES, (k + 1) * A_TILES) for k in range(A_MATS)]
    spans += [(R_WI + k * W_TILES, R_WI + (k + 1) * W_TILES) for k in range(W_MATS)]
    spans += [(R_WO, R_ALL)]
    sub = lax.broadcasted_iota(jnp.int32, (8, LANES), 0)
    lane = lax.broadcasted_iota(jnp.int32, (8, LANES), 1)
    levels = jnp.zeros((8, LANES), jnp.float32)
    ratios = jnp.zeros((8, LANES), jnp.float32)
    for k, (lo, hi) in enumerate(spans):
        levels = jnp.where(sub == k, total(rows[lo:hi, :]), levels)
        ratios = jnp.where(sub == k, total(ratio[lo:hi, :]), ratios)
    params = jnp.where(sub == lane, tot[S_PARAM : S_PARAM + 1, :], 0.0)
    levels = jnp.sum(levels, axis=1, keepdims=True)
    ratios = jnp.sum(ratios, axis=1, keepdims=True)
    params = jnp.sum(params, axis=1, keepdims=True)
    value = total(
        jnp.where(lane == sub, levels, 0.0)
        + jnp.where(lane == sub + 32, ratios, 0.0)
        + jnp.where(lane == sub + 64, params, 0.0)
    )
    for n in range(send.shape[0]):
        send[n] = value


def scaled_kernel(ta, gw, to, cols, after, ua, uw, uo, ac, wc, oc, done):
    done[...] = jnp.zeros_like(done)
    ac[...] = cols[0:A_MATS, :]
    for k, at, lo, hi in wi_places():
        wc[k : k + 1, lo:hi] = cols[at : at + 1, 0 : hi - lo]
    oc[...] = cols[C_WO : C_WO + 1, :]
    right = lax.rsqrt(cols[...])
    for k in range(A_MATS):
        column = as_column(right[k : k + 1, :])
        for t in range(A_TILES):
            tile = slice(t * LANES, (t + 1) * LANES)
            ua[k, tile, :] = ta[k, tile, :] * column
    column = as_column(right[C_WO : C_WO + 1, :])
    for t in range(O_TILES):
        tile = slice(t * LANES, (t + 1) * LANES)
        uo[tile, :] = to[tile, :] * column
    for k, at, lo, hi in wi_places():
        column = as_column(right[at : at + 1, :])[0 : hi - lo, :]
        for t in range(W_TILES):
            tile = slice(t * LANES, (t + 1) * LANES)
            uw[k, lo:hi, tile] = gw[k, lo:hi, tile] * column


def update_kernel(n_col, got, rows, ua, uw, uo, a, w, o, ar, wr, orr, va, vw, vo, var, vwr, sems):
    small = [(var, ar), (vwr, wr), (rows.at[R_WO:R_ALL, :], orr)]
    copies = [pltpu.make_async_copy(s, t, sems.at[i]) for i, (s, t) in enumerate(small)]
    for which, k, t, at in row_places():
        (var, vwr)[which][k : k + 1, t * LANES : (t + 1) * LANES] = rows[at : at + 1, :]
    for c in copies:
        c.start()

    def write(source, target):
        copies.append(pltpu.make_async_copy(source, target, sems.at[len(copies)]))
        copies[-1].start()

    left = lax.rsqrt(rows[0:R_ALL, :])
    tot = got[0]
    for n in range(1, got.shape[0]):
        tot = tot + got[n]
    sub = lax.broadcasted_iota(jnp.int32, (8, LANES), 0)
    lane = lax.broadcasted_iota(jnp.int32, (8, LANES), 1)
    levels, ratios, params = (
        jnp.sum(jnp.where(lane == sub + at, tot, 0.0), axis=1, keepdims=True) for at in (0, 32, 64)
    )
    sub = lax.broadcasted_iota(jnp.int32, (8, 1), 0)
    n_row = got.shape[0]
    full_rows = jnp.where(sub == N_MATS - 1, float(O_ROWS * n_row), float(A_ROWS * n_row))
    wide = (sub >= A_MATS) & (sub < A_MATS + W_MATS)
    full_cols = jnp.where(wide, float(W_COLS * n_col), float(LANES * n_col))
    count = full_rows * full_cols
    level = levels / full_rows
    dir_rms = jnp.sqrt(level * ratios / count)
    param_rms = jnp.sqrt(params / count)
    factor = -RHO * param_rms / jnp.maximum(1.0, dir_rms) * jnp.sqrt(level)
    for k in range(W_MATS):
        f = factor[A_MATS + k : A_MATS + k + 1, :]
        scale = [left[R_WI + k * W_TILES + t : R_WI + k * W_TILES + t + 1, :] * f for t in range(W_TILES)]
        for lo, hi in ((0, W_COLS // 2), (W_COLS // 2, W_COLS)):
            for t in range(W_TILES):
                tile = slice(t * LANES, (t + 1) * LANES)
                vw[k, lo:hi, tile] = uw[k, lo:hi, tile] * scale[t]
            write(vw.at[k, lo:hi], w.at[k, lo:hi])
    for k in range(A_MATS):
        f = factor[k : k + 1, :]
        for t in range(A_TILES):
            at = k * A_TILES + t
            tile = slice(t * LANES, (t + 1) * LANES)
            va[k, tile, :] = (ua[k, tile, :] * (left[at : at + 1, :] * f)).T
            if t % 2:
                half = slice((t - 1) * LANES, (t + 1) * LANES)
                write(va.at[k, half], a.at[k, half])
    f = factor[N_MATS - 1 : N_MATS, :]
    for t in range(O_TILES):
        at = R_WO + t
        tile = slice(t * LANES, (t + 1) * LANES)
        vo[tile, :] = (uo[tile, :] * (left[at : at + 1, :] * f)).T
        if t % 2:
            half = slice((t - 1) * LANES, (t + 1) * LANES)
            write(vo.at[half], o.at[half])
    for c in copies:
        c.wait()


def exchange(x, axes):
    return lax.all_to_all(x, axes, 0, 0)


def quad(x, axis, pairings):
    indices = range(lax.axis_size(axis))
    got = [lax.ppermute(x, axis, [(i, i ^ bits) for i in indices]) for bits in pairings]
    return [x] + got[::-1]


def mirror(x, axis):
    n = lax.axis_size(axis)
    return lax.ppermute(x, axis, [(i, n - 1 - i) for i in range(n)])


def shards(
    attn_grad,
    attn_param,
    attn_rows,
    attn_cols,
    wi_grad,
    wi_param,
    wi_rows,
    wi_cols,
    wo_grad,
    wo_param,
    wo_rows,
    wo_cols,
):
    n_row, n_col = lax.axis_size(ROW), lax.axis_size(COL)
    wi_grad = jnp.swapaxes(wi_grad, 1, 2)
    wi_param = jnp.swapaxes(wi_param, 1, 2)
    blocks = ((A_MATS, A_ROWS, LANES), (W_MATS, W_COLS, W_ROWS), (O_ROWS, LANES))
    held = [vmem(*b) for b in blocks]
    sems = pltpu.SemaphoreType.DMA((N_MATS,))
    send, ga, gw, go = call(
        load_kernel,
        [f32(n_row, 1, C_SENT * LANES)] + held,
        [ANYWHERE] * 3,
        [WHOLE] * 4,
        [vmem(C_ALL, LANES), sems],
        bytes_accessed=3 << 20,
    )(far(attn_grad), far(wi_grad), far(wo_grad))
    got = exchange(send, ROW[::-1])
    ga, gw, go = here(ga), here(gw), here(go)
    ta, to, row_sums, old_rows, old_cols = call(
        rows_kernel,
        [held[0], held[2], vmem(40, LANES), vmem(40, LANES), vmem(C_ALL, LANES)],
        [WHOLE] * 3 + [ANYWHERE] * 3 + [WHOLE] * 6,
        [WHOLE] * 5,
        held + [vmem(8, LANES), sems],
        bytes_accessed=6 << 20,
        aliases={0: 0, 2: 1},
    )(
        ga,
        gw,
        go,
        far(attn_param),
        far(wi_param),
        far(wo_param),
        attn_rows,
        wi_rows,
        wo_rows.reshape(O_TILES, LANES),
        attn_cols,
        wi_cols,
        wo_cols.reshape(1, LANES),
    )
    ta, to = here(ta), here(to)
    send, cols = call(
        cols_kernel,
        [f32(S_ALL, LANES), vmem(C_ALL, LANES)],
        [WHOLE] * 6,
        [WHOLE] * 2,
        [vmem(S_ALL, LANES)],
        bytes_accessed=3 << 20,
    )(got, here(old_cols), here(row_sums), ta, gw, to)
    got = quad(send, "z", (3, 2, 1))
    send = call(sum4_kernel, f32(S_ALL, LANES), [WHOLE] * 4, WHOLE)(*got)
    got = quad(send, "x", (2, 3, 1))
    ua, uw, uo, attn_cols_new, wi_cols_new, wo_cols_new, done = call(
        scaled_kernel,
        held + [f32(A_MATS, LANES), f32(W_MATS, W_COLS), f32(1, LANES), vmem(8, LANES)],
        [WHOLE] * 4 + [ANYWHERE],
        [WHOLE] * 7,
        bytes_accessed=6 << 20,
        aliases={0: 0, 1: 1, 2: 2},
    )(ta, gw, to, here(cols), send)
    send = call(sum4_and_kernel, f32(S_ALL, LANES), [ANYWHERE] + [WHOLE] * 4, WHOLE)(here(done), *got)
    got = mirror(send, "z")
    send, rows = call(
        lambda *refs: new_rows_kernel(n_col, *refs),
        [f32(n_row, 1, LANES), vmem(40, LANES)],
        [WHOLE] * 3,
        [WHOLE] * 2,
        [vmem(S_ALL, LANES), vmem(R_ALL, LANES)],
    )(here(old_rows), send, got)
    got = exchange(send, ROW[::-1])
    attn_update, wi_update, wo_update, attn_rows_new, wi_rows_new, wo_rows_new = call(
        lambda *refs: update_kernel(n_col, *refs),
        [hbm(*b) for b in blocks] + [hbm(A_MATS, A_ROWS), hbm(W_MATS, W_ROWS), hbm(O_TILES, LANES)],
        [WHOLE] * 5,
        [ANYWHERE] * 6,
        held + [vmem(A_MATS, A_ROWS), vmem(W_MATS, W_ROWS), pltpu.SemaphoreType.DMA((N_WRITES,))],
        bytes_accessed=3 << 20,
    )(got, here(rows), here(ua), here(uw), here(uo))
    return (
        attn_update,
        attn_rows_new,
        attn_cols_new,
        jnp.swapaxes(wi_update, 1, 2),
        wi_rows_new,
        wi_cols_new,
        wo_update,
        wo_rows_new.reshape(O_ROWS),
        wo_cols_new.reshape(LANES),
    )


def solution(mesh):
    fine = Mesh(mesh.devices.reshape(4, 2, 4, 8), ROW + COL)
    big, row, col = P(None, ROW, COL), P(None, ROW), P(None, COL)
    return jax.shard_map(
        shards,
        mesh=fine,
        in_specs=(big, big, row, col, big, big, row, col, P(ROW, COL), P(ROW, COL), P(ROW), P(COL)),
        out_specs=(big, row, col, big, row, col, P(ROW, COL), P(ROW), P(COL)),
        check_vma=False,
    )
```
